32 devices in a mesh: pipe: 4 (over z), head: 8 (over y, x, core).
Axes of the slice: x: 2, y: 2, z: 4, core: 2. Of those that a mesh axis runs over, the one named last changes fastest.
Arguments:
- hidden: bfloat16 [2, 64, 8192], P(None, 'head'), may hold values from -6 to 6
- norm_gain: float32 [4, 8192], P('pipe'), may hold values from 0.1 to 1.9
- w_x: bfloat16 [4, 8192, 16384], P('pipe', None, 'head'), may hold values from -0.0625 to 0.0625
- w_bc: bfloat16 [4, 8192, 4096], P('pipe', None, 'head'), may hold values from -0.03125 to 0.03125
- w_dt: bfloat16 [4, 8192, 256], P('pipe', None, 'head'), may hold values from -0.0625 to 0.0625
- conv_x: float32 [4, 4, 16384], P('pipe', None, 'head'), may hold values from -3 to 3
- conv_bc: float32 [4, 4, 4096], P('pipe'), may hold values from -3 to 3
- dt_bias: float32 [4, 256], P('pipe', 'head'), may hold values from -3 to 0.5
- a_rate: float32 [4, 256], P('pipe', 'head'), may hold values from 0.002 to 0.2
- d_skip: float32 [4, 256], P('pipe', 'head'), may hold values from 0.5 to 1.5
- w_out: bfloat16 [4, 16384, 8192], P('pipe', 'head'), may hold values from -0.046875 to 0.046875
- ssm_init: float32 [4, 256, 64, 256], P('pipe', 'head'), may hold values from -0.6 to 0.6
- conv_x_init: float32 [4, 3, 16384], P('pipe', None, 'head'), may hold values from -6 to 6
- conv_bc_init: float32 [4, 3, 4096], P('pipe'), may hold values from -3 to 3
Outputs:
- segment_out: bfloat16 [4, 2, 64, 8192], P('pipe', None, 'head')
- state_out: float32 [4, 256, 64, 256], P('pipe', 'head')
The draws below stay inside these ranges and needn't reach their ends.
All inputs are finite; a program needn't handle non-finite values.
Results may differ from the reference program's by a relative error of at most 0.039.
Values may be sent and summed in bfloat16 or wider, within the bound.
No kernel may reach another device: no remote copies, remote signals or barrier semaphores. Data moves between devices by JAX's collectives and lax.ppermute only.
A program may use at most 192 MiB of HBM per device.

```python
import math
import jax
import jax.numpy as jnp
from jax import lax

D = 8192
HEADS = 256
HEAD_DIM = 64
STATE = 256
GROUPS = 8
CONV = 4
BLOCK = 64
MICRO = 2
INNER = 16384
N_PIPE = 4
N_HEAD = 8


def level_of(own_key, dims, cuts, smallest, largest):
    factor_of, own = 1.0, jax.random.fold_in(own_key, 6)
    for position, shards_of in cuts:
        draws = jnp.exp(jax.random.uniform(jax.random.fold_in(own, position), (shards_of,), jnp.float32, smallest / len(cuts), largest / len(cuts)))
        factor_of = factor_of * jnp.repeat(draws, dims[position] // shards_of).reshape([-1 if axis == position else 1 for axis in range(len(dims))])
    return factor_of


def bell_draw(rng, dims, width, most, cuts=(), kind=jnp.bfloat16):
    level = level_of(rng, dims, cuts, -0.22, 0.18) if cuts else 1.0
    values = jax.random.normal(rng, dims, jnp.float32) * width * level
    return jnp.minimum(jnp.maximum(values, -most), most).astype(kind)


def setup_inputs(seed: int = 0) -> dict:
    arg_keys = jax.random.split(jax.random.key(seed), 15)
    return {
        "hidden": bell_draw(arg_keys[0], (MICRO, BLOCK, D), 1.0, 6.0, ((1, 8),)),
        "norm_gain": jnp.clip(1.0 + 0.18 * jax.random.normal(arg_keys[1], (N_PIPE, D), jnp.float32), 0.1, 1.9),
        "w_x": bell_draw(arg_keys[2], (N_PIPE, D, INNER), D ** -0.5, 0.0625, ((0, 4), (2, 8))),
        "w_bc": bell_draw(arg_keys[3], (N_PIPE, D, 2 * GROUPS * STATE), (4 * D) ** -0.5, 0.03125, ((0, 4), (2, 8))),
        "w_dt": bell_draw(arg_keys[4], (N_PIPE, D, HEADS), D ** -0.5, 0.0625, ((0, 4), (2, 8))),
        "conv_x": bell_draw(arg_keys[5], (N_PIPE, CONV, INNER), CONV ** -0.5, 3.0, ((0, 4), (2, 8)), jnp.float32),
        "conv_bc": bell_draw(arg_keys[6], (N_PIPE, CONV, 2 * GROUPS * STATE), CONV ** -0.5, 3.0, ((0, 4),), jnp.float32),
        "dt_bias": jnp.clip(-3.0 + 3.5 * jax.random.uniform(arg_keys[7], (N_PIPE, HEADS), jnp.float32) ** level_of(arg_keys[7], (N_PIPE, HEADS), ((0, 4), (1, 8)), -0.2, 0.2), -3.0, 0.5),
        "a_rate": jnp.clip(jnp.exp(math.log(0.2) - 4.6051702 * jax.random.uniform(arg_keys[8], (N_PIPE, HEADS), jnp.float32) ** level_of(arg_keys[8], (N_PIPE, HEADS), ((0, 4), (1, 8)), -0.2, 0.2)), 0.002, 0.2),
        "d_skip": jnp.clip(0.5 + 1.0 * jax.random.uniform(arg_keys[9], (N_PIPE, HEADS), jnp.float32) ** level_of(arg_keys[9], (N_PIPE, HEADS), ((0, 4), (1, 8)), -0.2, 0.2), 0.5, 1.5),
        "w_out": bell_draw(arg_keys[10], (N_PIPE, INNER, D), INNER ** -0.5, 0.046875, ((0, 4), (1, 8))),
        "ssm_init": bell_draw(arg_keys[11], (N_PIPE, HEADS, HEAD_DIM, STATE), 0.1, 0.6, ((0, 4), (1, 8)), jnp.float32),
        "conv_x_init": bell_draw(arg_keys[12], (N_PIPE, CONV - 1, INNER), 1.0, 6.0, ((0, 4), (2, 8)), jnp.float32),
        "conv_bc_init": bell_draw(arg_keys[13], (N_PIPE, CONV - 1, 2 * GROUPS * STATE), 0.5, 3.0, ((0, 4),), jnp.float32),
    }


def rms_rows(block_in, norm_weight):
    floats = block_in.astype(jnp.float32)
    scaled = floats * lax.rsqrt(lax.optimization_barrier(jnp.mean(floats * floats, axis=-1, keepdims=True)) + 1e-05)
    return (scaled * norm_weight[None, :]).astype(jnp.bfloat16)

def causal_conv(tail_rows, values, taps):
    padded = jnp.concatenate([tail_rows, values], axis=0)
    length = values.shape[0]
    conv_sum = taps[0][None, :] * padded[0:length]
    for offset in range(1, taps.shape[0]):
        conv_sum = conv_sum + taps[offset][None, :] * padded[offset:offset + length]
    return (jax.nn.silu(conv_sum), padded[length:])

def scan_block(values, b_heads, c_heads, step_size, decay_rate, skip_gain, ssm_state):
    highest = lax.Precision.HIGHEST
    log_decay = jnp.cumsum(-step_size * decay_rate[None, :], axis=0)
    length = values.shape[0]
    causal = (jnp.arange(length)[:, None] >= jnp.arange(length)[None, :])[:, :, None]
    gap_log = log_decay[:, None, :] - log_decay[None, :, :]
    decay_pairs = jnp.where(causal, jnp.exp(jnp.where(causal, gap_log, 0.0)), 0.0)
    scores = jnp.einsum('thn,shn->tsh', c_heads, b_heads, precision=highest)
    pair_weight = scores * decay_pairs * step_size[None, :, :]
    within = jnp.einsum('tsh,shp->thp', pair_weight, values, precision=highest)
    carried = jnp.exp(log_decay)[:, :, None] * jnp.einsum('thn,hpn->thp', c_heads, ssm_state, precision=highest)
    mixed_out = within + carried + skip_gain[None, :, None] * values
    end_log = log_decay[-1]
    to_end = jnp.exp(end_log[None, :] - log_decay) * step_size
    new_state = jnp.exp(end_log)[:, None, None] * ssm_state + jnp.einsum('sh,shp,shn->hpn', to_end, values, b_heads, precision=highest)
    return (mixed_out, new_state)

def reference(hidden, norm_gain, w_x, w_bc, w_dt, conv_x, conv_bc, dt_bias, a_rate, d_skip, w_out, ssm_init, conv_x_init, conv_bc_init):
    group_of = jnp.arange(HEADS) // (HEADS // GROUPS)
    share = INNER // N_HEAD
    current = [hidden[block_index] for block_index in range(MICRO)]
    layer_outs = []
    layer_states = []
    for layer_index in range(N_PIPE):
        ssm_state = ssm_init[layer_index]
        tail_x = conv_x_init[layer_index]
        tail_bc = conv_bc_init[layer_index]
        produced = []
        for block_index in range(MICRO):
            block_in = current[block_index]
            normed = rms_rows(block_in, norm_gain[layer_index])
            x_proj = jnp.dot(normed, w_x[layer_index], preferred_element_type=jnp.float32)
            bc_proj = jnp.dot(normed, w_bc[layer_index], preferred_element_type=jnp.float32).astype(jnp.bfloat16)
            dt_raw = jnp.dot(normed, w_dt[layer_index], preferred_element_type=jnp.float32)
            x_conv, tail_x = causal_conv(tail_x, x_proj, conv_x[layer_index])
            bc_conv, tail_bc = causal_conv(tail_bc, bc_proj.astype(jnp.float32), conv_bc[layer_index])
            step_size = jax.nn.softplus(dt_raw + dt_bias[layer_index][None, :])
            grouped = bc_conv.reshape(BLOCK, 2, STATE, GROUPS)
            b_heads = jnp.transpose(grouped[:, 0][:, :, group_of], (0, 2, 1))
            c_heads = jnp.transpose(grouped[:, 1][:, :, group_of], (0, 2, 1))
            mixed, ssm_state = scan_block(x_conv.reshape(BLOCK, HEADS, HEAD_DIM), b_heads, c_heads, step_size, a_rate[layer_index], d_skip[layer_index], ssm_state)
            mixed_bf = mixed.reshape(BLOCK, INNER).astype(jnp.bfloat16)
            summed = jnp.zeros((BLOCK, D), jnp.float32)
            for part_index in range(N_HEAD):
                partial_value = jnp.dot(mixed_bf[:, part_index * share:(part_index + 1) * share], w_out[layer_index][part_index * share:(part_index + 1) * share], preferred_element_type=jnp.float32)
                rounded = lax.optimization_barrier(partial_value.astype(jnp.bfloat16))
                summed = summed + rounded.astype(jnp.float32)
            produced.append((block_in.astype(jnp.float32) + summed).astype(jnp.bfloat16))
        layer_outs.append(jnp.stack(produced, axis=0))
        layer_states.append(ssm_state)
        current = produced
    return (jnp.stack(layer_outs, axis=0), jnp.stack(layer_states, axis=0))
```

```python
import functools

import jax
import jax.numpy as jnp
from jax import lax
from jax.experimental import pallas as pl
from jax.experimental.pallas import tpu as pltpu
from jax.sharding import PartitionSpec as P

STATE = 256
GROUPS = 8
MIB = 1 << 20
BF = jnp.bfloat16
F32 = jnp.float32
HIGHEST = lax.Precision.HIGHEST
VMEM_LIMIT = 40 * MIB
OUT_PARTS = 2


def whole(shape):
    return pl.BlockSpec(shape, lambda *_: (0,) * len(shape))


def cost(flops, nbytes):
    return pl.CostEstimate(flops=int(flops), bytes_accessed=int(nbytes), transcendentals=0)


def params():
    return pltpu.CompilerParams(vmem_limit_bytes=VMEM_LIMIT)


def dot(a, b, **kw):
    return jnp.dot(a, b, preferred_element_type=F32, **kw)


def chip_ring(chips):
    return [0, 1, 3, 2] if chips == 4 else list(range(chips))


def core_swap(value):
    count = lax.axis_size("head")
    return lax.ppermute(value, "head", [(i, i ^ 1) for i in range(count)])


def ring_shift(value, steps):
    chips = lax.axis_size("head") // 2
    ring = chip_ring(chips)
    pairs = [
        (2 * ring[i] + c, 2 * ring[(i + steps) % chips] + c) for i in range(chips) for c in range(2)
    ]
    return lax.ppermute(value, "head", pairs)


def next_segment(value, tick):
    count = lax.axis_size("pipe")
    pairs = []
    for low in range(tick % 2, count - 1, 2):
        pairs += [(low, low + 1), (low + 1, low)]
    return lax.ppermute(value, "pipe", pairs)


def relative_devices(sign):
    head = lax.axis_index("head")
    chips = lax.axis_size("head") // 2
    ring = chip_ring(chips)
    place = [ring.index(chip) for chip in range(chips)]
    mine = jnp.array(place, jnp.int32)[head // 2]
    steps = (mine + sign * jnp.arange(chips)) % chips
    chip = jnp.array(ring, jnp.int32)[steps]
    core = (head % 2) ^ jnp.arange(2)
    return 2 * chip[None, :] + core[:, None]


def first_kernel(own_ref, other_ref, order_ref, same_pick_ref, other_pick_ref, wbc_ref, wdt_ref,
                 normed_ref, dt_ref, same_ref, cross_ref):
    step = pl.program_id(0)
    half = own_ref.shape[0]
    width = own_ref.shape[1]
    block = 512

    @pl.when(step == 0)
    def _():
        @pl.loop(0, width // block)
        def _(i):
            cols = pl.ds(pl.multiple_of(i * block, block), block)
            normed_ref[:, cols] = (
                dot(order_ref[:, :half], own_ref[:, cols])
                + dot(order_ref[:, half:], other_ref[:, cols])
            ).astype(BF)

        dt_ref[...] = dot(normed_ref[...], wdt_ref[...])

    part = dot(normed_ref[...], wbc_ref[...]).astype(BF)
    same = dot(part, same_pick_ref[...]).astype(BF)
    cross = dot(part, other_pick_ref[...]).astype(BF)

    @pl.when(step == 0)
    def _():
        same_ref[...] = same
        cross_ref[...] = cross

    @pl.when(step > 0)
    def _():
        same_ref[...] += same
        cross_ref[...] += cross


def project_first(own, other, order, same_pick, cross_pick, w_bc, w_dt):
    width, bc_cols = w_bc.shape
    rows = order.shape[0]
    heads = w_dt.shape[1]
    out_cols = same_pick.shape[1]
    block = min(256, bc_cols)
    return pl.pallas_call(
        first_kernel,
        grid=(bc_cols // block,),
        in_specs=[
            whole(own.shape),
            whole(other.shape),
            whole(order.shape),
            pl.BlockSpec((block, out_cols), lambda i: (i, 0)),
            pl.BlockSpec((block, out_cols), lambda i: (i, 0)),
            pl.BlockSpec((width, block), lambda i: (0, i)),
            whole(w_dt.shape),
        ],
        out_specs=[whole((rows, width)), whole((rows, heads)), whole((rows, out_cols)), whole((rows, out_cols))],
        out_shape=[
            jax.ShapeDtypeStruct((rows, width), BF),
            jax.ShapeDtypeStruct((rows, heads), F32),
            jax.ShapeDtypeStruct((rows, out_cols), BF),
            jax.ShapeDtypeStruct((rows, out_cols), BF),
        ],
        compiler_params=params(),
        cost_estimate=cost(2 * rows * width * (bc_cols + heads), 2 * w_bc.size + 4 * rows * width),
    )(own, other, order, same_pick, cross_pick, w_bc, w_dt)


def inner_kernel(normed_ref, w_ref, x_ref):
    x_ref[...] = dot(normed_ref[...], w_ref[...])


def project_inner(normed, w_x):
    rows, width = normed.shape
    cols = w_x.shape[1]
    block = min(256, cols)
    return pl.pallas_call(
        inner_kernel,
        grid=(cols // block,),
        in_specs=[whole(normed.shape), pl.BlockSpec((width, block), lambda i: (0, i))],
        out_specs=pl.BlockSpec((rows, block), lambda i: (0, i)),
        out_shape=jax.ShapeDtypeStruct((rows, cols), F32),
        compiler_params=params(),
        cost_estimate=cost(2 * rows * width * cols, 2 * w_x.size + 2 * normed.size),
    )(normed, w_x)


def conv_silu(pad_ref, tail_ref, taps_ref):
    taps, rows = taps_ref.shape[0], pad_ref.shape[0] - 8
    pad_ref[8 - (taps - 1):8, :] = tail_ref[...]
    total = taps_ref[0:1, :] * pad_ref[pl.ds(9 - taps, rows), :]
    for k in range(1, taps):
        total = total + taps_ref[k:k + 1, :] * pad_ref[pl.ds(9 - taps + k, rows), :]
    return total * jax.nn.sigmoid(total)


def scan_kernel(x_ref, bc_ref, dt_ref, place_ref, spread_ref, tail_x_ref, taps_x_ref, tail_bc_ref, taps_bc_ref,
                bias_ref, rate_ref, skip_ref, state_ref, y_ref, weighted_ref, b_ref, end_ref,
                pad_x, pad_bc, scaled):
    rows, channels = x_ref.shape
    heads = dt_ref.shape[1]
    dim = channels // heads
    half = bc_ref.shape[1] // 2

    pad_bc[8:, :] = dot(bc_ref[...], place_ref[...])
    bc = conv_silu(pad_bc, tail_bc_ref, taps_bc_ref)
    b_mat, c_mat = bc[:, :half], bc[:, half:]
    b_bf, c_bf = b_mat.astype(BF), c_mat.astype(BF)
    b_ref[...] = b_bf
    contract = (((1,), (1,)), ((), ()))
    scores = lax.dot_general(c_mat, b_mat, contract, precision=HIGHEST, preferred_element_type=F32)
    t_ids = lax.broadcasted_iota(jnp.int32, (rows, rows), 0)
    s_ids = lax.broadcasted_iota(jnp.int32, (rows, rows), 1)
    causal = t_ids >= s_ids
    scores = jnp.where(causal, scores, 0.0)

    raw = dt_ref[...] + bias_ref[...]
    step = jnp.maximum(raw, 0.0) + jnp.log1p(jnp.exp(-jnp.abs(raw)))
    log_decay = dot(causal.astype(F32), -step * rate_ref[...], precision=HIGHEST)
    end_log = log_decay[rows - 1:rows, :]
    end_ref[...] = jnp.exp(end_log)
    spread = spread_ref[...]
    step_full = dot(step, spread, precision=HIGHEST)
    to_end_full = dot(jnp.exp(end_log - log_decay), spread, precision=HIGHEST)
    decay_full = dot(jnp.exp(log_decay), spread, precision=HIGHEST)
    log_rows = log_decay.T

    pad_x[8:, :] = x_ref[...]
    x_conv = conv_silu(pad_x, tail_x_ref, taps_x_ref)
    stepped = x_conv * step_full
    scaled[...] = stepped.astype(BF)
    weighted_ref[...] = (stepped * to_end_full).astype(BF)
    state = state_ref[...].reshape(channels, half).astype(BF)
    carried = lax.dot_general(c_bf, state, contract, preferred_element_type=F32)
    base = carried * decay_full + skip_ref[...] * x_conv
    for j in range(heads):
        gap = jnp.minimum(log_decay[:, j:j + 1] - log_rows[j:j + 1, :], 0.0)
        weight = (scores * jnp.exp(gap)).astype(BF)
        cols = slice(j * dim, (j + 1) * dim)
        y_ref[:, cols] = (base[:, cols] + dot(weight, scaled[:, cols])).astype(BF)


def scan(x_proj, bc, dt_raw, place, spread, tail_x, taps_x, tail_bc, taps_bc, bias, rate, skip, state):
    rows, channels = x_proj.shape
    heads = dt_raw.shape[1]
    half = bc.shape[1] // 2
    args = (x_proj, bc, dt_raw, place, spread, tail_x, taps_x, tail_bc, taps_bc, bias, rate, skip, state)
    shapes = [
        jax.ShapeDtypeStruct((rows, channels), BF),
        jax.ShapeDtypeStruct((rows, channels), BF),
        jax.ShapeDtypeStruct((rows, half), BF),
        jax.ShapeDtypeStruct((1, heads), F32),
    ]
    return pl.pallas_call(
        scan_kernel,
        in_specs=[whole(a.shape) for a in args],
        out_specs=[whole(s.shape) for s in shapes],
        out_shape=shapes,
        grid=(1,),
        scratch_shapes=[
            pltpu.VMEM((rows + 8, channels), F32),
            pltpu.VMEM((rows + 8, 2 * half), F32),
            pltpu.VMEM((rows, channels), BF),
        ],
        compiler_params=params(),
        cost_estimate=cost(2 * rows * channels * (rows + half), 8 * rows * channels + 4 * state.size),
    )(*args)


def state_kernel(active_ref, end_ref, weighted_ref, b_ref, state_ref, kept_ref, out_ref):
    heads, dim, width = state_ref.shape

    @pl.when(active_ref[0] == 1)
    def _():
        added = lax.dot_general(
            weighted_ref[...], b_ref[...], (((0,), (0,)), ((), ())), preferred_element_type=F32
        )
        for j in range(heads):
            out_ref[j] = end_ref[0, j] * state_ref[j] + added[j * dim:(j + 1) * dim, :]

    @pl.when(active_ref[0] == 0)
    def _():
        out_ref[...] = kept_ref[...]


def state_update(active, end, weighted, b_mat, state, kept):
    smem = pl.BlockSpec(memory_space=pltpu.SMEM)
    return pl.pallas_call(
        state_kernel,
        grid=(1,),
        in_specs=[smem, smem, whole(weighted.shape), whole(b_mat.shape), whole(state.shape), whole(state.shape)],
        out_specs=whole(state.shape),
        out_shape=jax.ShapeDtypeStruct(state.shape, F32),
        compiler_params=params(),
        cost_estimate=cost(2 * weighted.size * b_mat.shape[1], 12 * state.size),
    )(active, end, weighted, b_mat, state, kept)


def out_kernel(y_ref, order_ref, w_ref, p_ref, sorted_ref):
    @pl.when(pl.program_id(0) == 0)
    def _():
        sorted_ref[...] = dot(order_ref[...], y_ref[...]).astype(BF)

    p_ref[...] = dot(sorted_ref[...], w_ref[...]).astype(BF)


def project_out(y, order, w_out, part, parts):
    rows, depth = y.shape
    cols = w_out.shape[1] // parts
    block = min(1024, cols)
    first = part * (cols // block)
    return pl.pallas_call(
        out_kernel,
        grid=(cols // block,),
        in_specs=[whole(y.shape), whole(order.shape), pl.BlockSpec((depth, block), lambda i: (0, first + i))],
        out_specs=pl.BlockSpec((rows, block), lambda i: (0, i)),
        out_shape=jax.ShapeDtypeStruct((rows, cols), BF),
        scratch_shapes=[pltpu.VMEM((rows, depth), BF)],
        compiler_params=params(),
        cost_estimate=cost(2 * rows * depth * cols, 2 * depth * cols),
    )(y, order, w_out)


def rms_rows(rows_in, gain):
    floats = rows_in.astype(F32)
    scaled = floats * lax.rsqrt(jnp.mean(floats * floats, axis=-1, keepdims=True) + 1e-05)
    return (scaled * gain[None, :]).astype(BF)


def per_device(hidden, norm_gain, w_x, w_bc, w_dt, conv_x, conv_bc, dt_bias, a_rate, d_skip, w_out,
               ssm_init, conv_x_init, conv_bc_init):
    segment = lax.axis_index("pipe")
    segments = lax.axis_size("pipe")
    head = lax.axis_index("head")
    devices = lax.axis_size("head")
    chips = devices // 2
    micro, local, width = hidden.shape
    own_rows = micro * local
    rows = own_rows * devices
    half = rows // 2
    local_heads = dt_bias.shape[1]
    channels = w_x.shape[2]
    bc_cols = w_bc.shape[2]
    span = bc_cols // GROUPS

    sources = relative_devices(-1)
    targets = relative_devices(1)

    def token_of(devs):
        ids = jnp.arange(micro)[:, None] * (local * devices) + jnp.arange(local)[None, :]
        return (devs[:, :, None, None] * local + ids).reshape(-1)

    tokens = jnp.arange(rows)
    gather_order = (tokens[:, None] == token_of(sources)[None, :]).astype(BF)
    scatter_order = (token_of(targets)[:, None] == tokens[None, :]).astype(BF)
    group_of = targets * GROUPS // devices
    lanes = jnp.arange(span) * GROUPS
    columns = jnp.arange(bc_cols)
    none = jnp.full((chips, span), -1)
    same_lane = jnp.stack([group_of[0][:, None] + lanes[None, :], none], axis=1).reshape(-1)
    cross_lane = jnp.stack([none, group_of[1][:, None] + lanes[None, :]], axis=1).reshape(-1)
    same_pick = (columns[:, None] == same_lane[None, :]).astype(BF)
    cross_pick = (columns[:, None] == cross_lane[None, :]).astype(BF)
    place_of = (sources.T[:, :, None] * span + jnp.arange(span)[None, None, :]).reshape(-1)
    place = (place_of[:, None] == jnp.arange(2 * STATE)[None, :]).astype(BF)
    spread = (jnp.arange(local_heads)[:, None] == (jnp.arange(channels) // (channels // local_heads))[None, :]).astype(F32)

    my_group = head * GROUPS // devices
    tail_bc = lax.dynamic_index_in_dim(conv_bc_init[0].reshape(-1, 2 * STATE, GROUPS), my_group, 2, keepdims=False)
    taps_bc = lax.dynamic_index_in_dim(conv_bc[0].reshape(-1, 2 * STATE, GROUPS), my_group, 2, keepdims=False)
    skip = jnp.repeat(d_skip[0], channels // local_heads)[None, :]

    current = hidden.reshape(own_rows, width)
    out_rows = jnp.zeros((own_rows, width), BF)
    state_out = ssm_init[0]
    for tick in range(segments):
        active = segment == tick
        flag = active.astype(jnp.int32).reshape(1)
        normed = rms_rows(current, norm_gain[0])
        pieces = [normed] + [ring_shift(normed, s) for s in range(1, chips)]
        gathered = jnp.concatenate(pieces, axis=0)
        gathered_other = core_swap(gathered)
        normed_all, dt_raw, bc_same, bc_cross = project_first(
            gathered, gathered_other, gather_order, same_pick, cross_pick, w_bc[0], w_dt[0]
        )
        bc_pair = bc_same + core_swap(bc_cross)
        bc_parts = [bc_pair[:, s * 2 * span:(s + 1) * 2 * span] for s in range(chips)]
        bc_parts = [bc_parts[0]] + [ring_shift(bc_parts[s], s) for s in range(1, chips)]
        bc_rel = jnp.concatenate(bc_parts, axis=1)
        x_proj = project_inner(normed_all, w_x[0])
        y, weighted, b_mat, end = scan(
            x_proj, bc_rel, dt_raw, place, spread, conv_x_init[0], conv_x[0], tail_bc, taps_bc,
            dt_bias, a_rate, skip, ssm_init[0],
        )
        state_out = state_update(flag, end, weighted, b_mat, ssm_init[0], state_out)
        new_parts = []
        part_cols = width // OUT_PARTS
        for part in range(OUT_PARTS):
            partial = project_out(y, scatter_order, w_out[0], part, OUT_PARTS)
            received = core_swap(partial[half:])
            pair = (partial[:half].astype(F32) + received.astype(F32)).astype(BF)
            moved = [ring_shift(pair[s * own_rows:(s + 1) * own_rows], s) for s in range(1, chips)]
            total = pair[:own_rows].astype(F32)
            for piece in moved:
                total = total + piece.astype(F32)
            new_parts.append(total)
        summed = jnp.concatenate(new_parts, axis=1)
        new_rows = (current.astype(F32) + summed).astype(BF)
        out_rows = jnp.where(active, new_rows, out_rows)
        if tick + 1 < segments:
            current = next_segment(new_rows, tick)
    return (out_rows.reshape(1, micro, local, width), state_out[None])


def solution(mesh):
    in_specs = (
        P(None, "head", None),
        P("pipe", None),
        P("pipe", None, "head"),
        P("pipe", None, "head"),
        P("pipe", None, "head"),
        P("pipe", None, "head"),
        P("pipe", None, None),
        P("pipe", "head"),
        P("pipe", "head"),
        P("pipe", "head"),
        P("pipe", "head", None),
        P("pipe", "head", None, None),
        P("pipe", None, "head"),
        P("pipe", None, None),
    )
    out_specs = (P("pipe", None, "head", None), P("pipe", "head", None, None))
    return jax.shard_map(
        per_device, mesh=mesh, in_specs=in_specs, out_specs=out_specs, check_vma=False
    )
```

```python
import functools

import jax
import jax.numpy as jnp
from jax import lax
from jax.experimental import pallas as pl
from jax.experimental.pallas import tpu as pltpu
from jax.sharding import PartitionSpec as P

STATE = 256
GROUPS = 8
MIB = 1 << 20
BF = jnp.bfloat16
F32 = jnp.float32
HIGHEST = lax.Precision.HIGHEST
SUM_LOADS = 4
HELD = 6
OUT_COLS = 1024
SCAN_MIB = 28


def whole(shape):
    return pl.BlockSpec(shape, lambda *_: (0,) * len(shape))


def cost(flops, nbytes):
    return pl.CostEstimate(flops=int(flops), bytes_accessed=int(nbytes), transcendentals=0)


def params(mib):
    return pltpu.CompilerParams(vmem_limit_bytes=mib * MIB)


def dot(a, b, **kw):
    return jnp.dot(a, b, preferred_element_type=F32, **kw)


def ring_place(chip, chips):
    return chip ^ (chip >> 1) if chips == 4 else chip


def core_swap(value):
    count = lax.axis_size("head")
    return lax.ppermute(value, "head", [(i, i ^ 1) for i in range(count)])


def ring_shift(value, steps):
    chips = lax.axis_size("head") // 2
    ring = [ring_place(i, chips) for i in range(chips)]
    pairs = [
        (2 * ring[i] + c, 2 * ring[(i + steps) % chips] + c) for i in range(chips) for c in range(2)
    ]
    return lax.ppermute(value, "head", pairs)


def next_segment(value, tick):
    count = lax.axis_size("pipe")
    pairs = []
    for low in range(tick % 2, count - 1, 2):
        pairs += [(low, low + 1), (low + 1, low)]
    return lax.ppermute(value, "pipe", pairs)


def bits(value, low, size):
    return (value >> (low.bit_length() - 1)) & (size - 1)


def iotas(rows, cols):
    return (
        lax.broadcasted_iota(jnp.int32, (rows, 1), 0),
        lax.broadcasted_iota(jnp.int32, (1, cols), 1),
    )


def device_at(head, distance, core, chips):
    place = (ring_place(head >> 1, chips) + distance) & (chips - 1)
    return 2 * ring_place(place, chips) + ((head & 1) ^ core)


def gather_order(head, rows, micro, local):
    devices = rows // (micro * local)
    chips = devices // 2
    time, place = iotas(rows, rows)
    device, block = bits(time, local, devices), bits(time, local * devices, micro)
    distance = (ring_place(head >> 1, chips) - ring_place(device >> 1, chips)) & (chips - 1)
    core = (device ^ head) & 1
    at = (((core * chips + distance) * micro) + block) * local + bits(time, 1, local)
    return (at == place).astype(F32).astype(BF)


def scatter_order(head, rows, micro, local):
    devices = rows // (micro * local)
    chips = devices // 2
    place, time = iotas(rows, rows)
    own = micro * local
    device = device_at(head, bits(place, own, chips), bits(place, own * chips, 2), chips)
    at = bits(place, local, micro) * (local * devices) + device * local + bits(place, 1, local)
    return (at == time).astype(F32).astype(BF)


def pick_columns(head, first, count, bc_cols, devices):
    chips, span = devices // 2, bc_cols // GROUPS
    column, sent = iotas(count, 2 * span * chips)
    device = device_at(head, bits(sent, 2 * span, chips), bits(sent, span, 2), chips)
    group = (device * GROUPS) >> (devices.bit_length() - 1)
    return (bits(sent, 1, span) * GROUPS + group == column + first).astype(F32).astype(BF)


def place_columns(head, core, devices):
    chips, span = devices // 2, 2 * STATE // devices
    sent, column = iotas(2 * STATE, 2 * STATE)
    device = device_at(head, -bits(sent, 2 * span, chips), core, chips)
    here = jnp.where(bits(sent, span, 2) == core, device * span + bits(sent, 1, span), -1)
    return (here == column).astype(F32).astype(BF)


def load_kernel(plan, go_ref, *refs):
    weights = max(p[0] for p in plan) + 1
    count = len(plan)
    sources, value_ref = refs[:weights], refs[weights]
    held, copy_ref, sems = refs[weights + 1:-2], refs[-2], refs[-1]
    copies = []
    for i, (which, index) in enumerate(plan):
        cols = held[i].shape[1]
        copies.append(
            pltpu.make_async_copy(sources[which].at[:, pl.ds(index * cols, cols)], held[i], sems.at[i])
        )
        copies[-1].start()

    @pl.when(go_ref[0] >= 0)
    def _():
        copy_ref[...] = value_ref[...]

    for i in range(count):
        copies[i].wait()


def load_beside(go, plan, value):
    if not plan:
        return [], value
    weights = []
    for weight, _, _ in plan:
        if not any(weight is w for w in weights):
            weights.append(weight)
    steps = [([weight is w for w in weights].index(True), index) for weight, _, index in plan]
    vmem = pl.BlockSpec(memory_space=pltpu.VMEM)
    nbytes = sum(2 * w.shape[0] * cols for w, cols, _ in plan)
    *held, value = pl.pallas_call(
        functools.partial(load_kernel, steps),
        in_specs=[pl.BlockSpec(memory_space=pltpu.SMEM)] + [pl.BlockSpec(memory_space=pl.ANY)] * len(weights) + [vmem],
        out_specs=[vmem] * (len(plan) + 1),
        out_shape=[pltpu.VMEM((w.shape[0], cols), w.dtype) for w, cols, _ in plan]
        + [jax.ShapeDtypeStruct(value.shape, value.dtype)],
        scratch_shapes=[pltpu.SemaphoreType.DMA((len(plan),))],
        compiler_params=params(2),
        cost_estimate=cost(0, nbytes),
    )(go, *[pltpu.with_memory_space_constraint(w, pltpu.HBM) for w in weights], value)
    return held, value


def first_kernel(count, micro, local, *refs):
    pieces, (go_ref, wdt_ref, wbc_ref, normed_ref, dt_ref, bc_ref, late, wdt, sems) = refs[:count], refs[count:]
    rows = pieces[0].shape[0]
    blocks, _, cols = late.shape

    def fetch(i):
        return pltpu.make_async_copy(wbc_ref.at[:, pl.ds(i * cols, cols)], late.at[i], sems.at[i])

    steps = pltpu.make_async_copy(wdt_ref, wdt, sems.at[blocks])
    steps.start()
    for i in range(blocks):
        fetch(i).start()

    @pl.when(go_ref[0] >= 0)
    def _():
        for i, piece in enumerate(pieces):
            normed_ref[i * rows:(i + 1) * rows, :] = piece[...]

    steps.wait()
    dt_ref[...] = lax.dot_general(
        normed_ref[...], wdt[...], (((1,), (1,)), ((), ())), preferred_element_type=F32
    )
    head = go_ref[0]
    all_rows = normed_ref.shape[0]
    devices = all_rows // (micro * local)
    gather = gather_order(head, all_rows, micro, local)
    total = jnp.zeros(bc_ref.shape, F32)
    for i in range(blocks):
        fetch(i).wait()
        part = dot(normed_ref[...], late[i]).astype(BF)
        part = dot(gather, part).astype(BF)
        total += dot(part, pick_columns(head, i * cols, cols, blocks * cols, devices))
    bc_ref[...] = total.astype(BF)


def project_first(go, pieces, micro, local, w_bc, w_dt):
    width, bc_cols = w_bc.shape
    rows = len(pieces) * pieces[0].shape[0]
    heads = w_dt.shape[0]
    vmem = pl.BlockSpec(memory_space=pltpu.VMEM)
    block = min(256, bc_cols)
    args = (*pieces, go, pltpu.with_memory_space_constraint(w_dt, pltpu.HBM), pltpu.with_memory_space_constraint(w_bc, pltpu.HBM))
    shapes = [
        jax.ShapeDtypeStruct((rows, width), BF),
        jax.ShapeDtypeStruct((rows, heads), F32),
        jax.ShapeDtypeStruct((rows, bc_cols // GROUPS * (rows // (micro * local))), BF),
    ]
    return pl.pallas_call(
        functools.partial(first_kernel, len(pieces), micro, local),
        in_specs=[vmem] * len(pieces) + [pl.BlockSpec(memory_space=pltpu.SMEM)]
        + [pl.BlockSpec(memory_space=pl.ANY)] * 2,
        out_specs=[vmem] * 3,
        out_shape=shapes,
        scratch_shapes=[
            pltpu.VMEM((bc_cols // block, width, block), BF),
            pltpu.VMEM(w_dt.shape, BF),
            pltpu.SemaphoreType.DMA((bc_cols // block + 1,)),
        ],
        compiler_params=params(12),
        cost_estimate=cost(2 * rows * width * (bc_cols + heads), 2 * w_bc.size),
    )(*args)


def held_kernel(count, go_ref, normed_ref, value_ref, *refs):
    held, (w_ref, x_ref, copy_ref, late, sems) = refs[:count], refs[count:]
    rest, _, cols = late.shape

    def fetch(i):
        return pltpu.make_async_copy(w_ref.at[:, pl.ds((count + i) * cols, cols)], late.at[i], sems.at[i])

    for i in range(rest):
        fetch(i).start()

    @pl.when(go_ref[0] >= 0)
    def _():
        copy_ref[...] = value_ref[...]
        for i, block_ref in enumerate(held):
            x_ref[:, i * cols:(i + 1) * cols] = dot(normed_ref[...], block_ref[...])

    for i in range(rest):
        fetch(i).wait()
        x_ref[:, (count + i) * cols:(count + i + 1) * cols] = dot(normed_ref[...], late[i])


def held_inner(go, normed, held, weight, block, value):
    rows, width = normed.shape
    cols = weight.shape[1]
    rest = cols // block - len(held)
    vmem = pl.BlockSpec(memory_space=pltpu.VMEM)
    return pl.pallas_call(
        functools.partial(held_kernel, len(held)),
        in_specs=[pl.BlockSpec(memory_space=pltpu.SMEM)] + [vmem] * (len(held) + 2) + [pl.BlockSpec(memory_space=pl.ANY)],
        out_specs=[vmem, vmem],
        out_shape=[jax.ShapeDtypeStruct((rows, cols), F32), jax.ShapeDtypeStruct(value.shape, value.dtype)],
        scratch_shapes=[pltpu.VMEM((rest, width, block), BF), pltpu.SemaphoreType.DMA((rest,))],
        compiler_params=params(4 + 2 * rest * width * block // MIB),
        cost_estimate=cost(2 * rows * width * cols, 2 * rows * width),
    )(go, normed, value, *[pltpu.with_memory_space_constraint(w, pltpu.VMEM) for w in held],
      pltpu.with_memory_space_constraint(weight, pltpu.HBM))


def join_kernel(*refs):
    lanes = refs[0].shape[1]
    for i, ref in enumerate(refs[:-1]):
        refs[-1][:, i * lanes:(i + 1) * lanes] = ref[...]


def join(parts):
    rows, lanes = parts[0].shape
    if lanes % 128:
        return jnp.concatenate(parts, axis=1)
    vmem = pl.BlockSpec(memory_space=pltpu.VMEM)
    return pl.pallas_call(
        join_kernel,
        in_specs=[vmem] * len(parts),
        out_specs=vmem,
        out_shape=jax.ShapeDtypeStruct((rows, lanes * len(parts)), parts[0].dtype),
        compiler_params=params(1),
        cost_estimate=cost(0, 4 * rows * lanes * len(parts)),
    )(*parts)


def conv_silu(pad_ref, const_ref, first, taps):
    rows, cols = pad_ref.shape[0] - 8, pad_ref.shape[1]
    pad_ref[8 - (taps - 1):8, :] = const_ref[first:first + taps - 1, :cols]
    at = first + taps - 1
    total = const_ref[at:at + 1, :cols] * pad_ref[pl.ds(9 - taps, rows), :]
    for k in range(1, taps):
        total = total + const_ref[at + k:at + k + 1, :cols] * pad_ref[pl.ds(9 - taps + k, rows), :]
    return total * jax.nn.sigmoid(total)


def in_time(order, groups_ref, group_rows, src_ref, dst_ref):
    rows = src_ref.shape[0]
    if group_rows % 8:
        dst_ref[8:, :] = dot(order.astype(F32), src_ref[...], precision=HIGHEST)
        return
    for g in range(rows // group_rows):
        start = pl.multiple_of(groups_ref[1 + g] * group_rows, group_rows)
        dst_ref[8 + g * group_rows:8 + (g + 1) * group_rows, :] = src_ref[pl.ds(start, group_rows), :]


def spread_exact(values, spread):
    high = values.astype(BF)
    rest = values - high.astype(F32)
    mid = rest.astype(BF)
    low = (rest - mid.astype(F32)).astype(BF)
    return dot(jnp.concatenate([high, mid, low], axis=1), spread)


def scan_kernel(micro, group_rows, slots, taps, groups_ref, flag_ref, x_ref, here_ref, over_ref, dt_ref, const_ref, state_ref,
                w_ref, _weighted, _b, _end, own_ref, other_ref, weighted_ref, b_ref, end_ref, pad_x, pad_bc, scaled, y_ref,
                sorted_ref, const, state_buf, weighted_buf, b_buf, end_buf, ring, sems, own_sems):
    pieces = (own_ref, other_ref)
    count = 0
    rows, channels = y_ref.shape
    active = flag_ref[0] == 1
    heads = dt_ref.shape[1]
    dim = channels // heads
    half = STATE
    devices = rows // (micro * group_rows)
    head = groups_ref[0]
    block = ring.shape[2]
    blocks = w_ref.shape[1] // block

    def fetch(i):
        slot = lax.rem(i, slots)
        cols = pl.ds(pl.multiple_of(i * block, block), block)
        return pltpu.make_async_copy(w_ref.at[:, cols], ring.at[slot], sems.at[slot])

    loads = [pltpu.make_async_copy(const_ref, const, own_sems.at[0]), pltpu.make_async_copy(state_ref, state_buf, own_sems.at[1])]
    for copy in loads:
        copy.start()
    for i in range(min(slots, blocks)):
        fetch(i).start()

    @pl.when(groups_ref[0] >= 0)
    def _():
        arrived = dot(here_ref[...], place_columns(head, 0, devices)) + dot(over_ref[...], place_columns(head, 1, devices))
        pad_bc[8:, :] = arrived
        gather = gather_order(head, rows, micro, group_rows)
        loads[0].wait()
        bc = conv_silu(pad_bc, const, 2 * taps, taps)
        b_mat, c_mat = bc[:, :half], bc[:, half:]
        b_bf, c_bf = b_mat.astype(BF), c_mat.astype(BF)
        b_buf[...] = b_bf
        contract = (((1,), (1,)), ((), ()))
        scores = lax.dot_general(c_mat, b_mat, contract, precision=HIGHEST, preferred_element_type=F32)
        t_ids = lax.broadcasted_iota(jnp.int32, (rows, rows), 0)
        s_ids = lax.broadcasted_iota(jnp.int32, (rows, rows), 1)
        causal = t_ids >= s_ids
        scores = jnp.where(causal, scores, 0.0)

        raw = dot(gather.astype(F32), dt_ref[...], precision=HIGHEST) + const[4 * taps - 1:4 * taps, :heads]
        step = jnp.maximum(raw, 0.0) + jnp.log1p(jnp.exp(-jnp.abs(raw)))
        log_decay = dot(causal.astype(F32), -step * const[4 * taps:4 * taps + 1, :heads], precision=HIGHEST)
        end_log = log_decay[rows - 1:rows, :]
        end_buf[...] = jnp.exp(end_log)
        part_head, channel = iotas(3 * heads, channels)
        spread = (bits(part_head, 1, heads) == (channel >> (dim.bit_length() - 1))).astype(F32).astype(BF)
        step_full = spread_exact(step, spread)
        to_end_full = spread_exact(jnp.exp(end_log - log_decay), spread)
        decay_full = spread_exact(jnp.exp(log_decay), spread)
        log_rows = log_decay.T

        in_time(gather, groups_ref, group_rows, x_ref, pad_x)
        x_conv = conv_silu(pad_x, const, 0, taps)
        stepped = x_conv * step_full
        scaled[...] = stepped.astype(BF)
        weighted_buf[...] = (stepped * to_end_full).astype(BF)
        for j in range(heads):
            gap = jnp.minimum(log_decay[:, j:j + 1] - log_rows[j:j + 1, :], 0.0)
            weight = (scores * jnp.exp(gap)).astype(BF)
            cols = slice(j * dim, (j + 1) * dim)
            pad_x[8:, cols] = const[2 * taps - 1:2 * taps, cols] * x_conv[:, cols] + dot(weight, scaled[:, cols])

        loads[1].wait()
        state = state_buf[...].reshape(channels, half).astype(BF)
        carried = lax.dot_general(c_bf, state, contract, preferred_element_type=F32)
        y_ref[...] = (pad_x[8:, :] + carried * decay_full).astype(BF)

    kept = [
        pltpu.make_async_copy(src, dst, own_sems.at[i])
        for i, (src, dst) in enumerate(((weighted_buf, weighted_ref), (b_buf, b_ref), (end_buf, end_ref)))
    ]

    @pl.when(active)
    def _():
        for copy in kept:
            copy.start()

    sorted_ref[...] = dot(scatter_order(head, rows, micro, group_rows), y_ref[...]).astype(BF)
    size = rows // 2

    @pl.loop(0, blocks)
    def _(i):
        fetch(i).wait()
        part = dot(sorted_ref[...], ring[lax.rem(i, slots)]).astype(BF)
        cols = pl.ds(pl.multiple_of(i * block, block), block)
        for q, piece in enumerate(pieces):
            piece[:, cols] = part[q * size:(q + 1) * size, :]

        @pl.when(i + slots < blocks)
        def _():
            fetch(i + slots).start()

    @pl.when(active)
    def _():
        for copy in kept:
            copy.wait()


def scan_and_out(micro, group_rows, taps, groups, flag, x_proj, here, over, dt_raw, const, state, old, w_out):
    rows, channels = x_proj.shape
    width = w_out.shape[1]
    block, slots = OUT_COLS, 4
    far = [pltpu.with_memory_space_constraint(a, pltpu.HBM) for a in (const, state, w_out, *old)]
    shapes = [jax.ShapeDtypeStruct((rows // 2, width), BF)] * 2 + [jax.ShapeDtypeStruct(o.shape, o.dtype) for o in old]
    vmem = pl.BlockSpec(memory_space=pltpu.VMEM)
    smem = pl.BlockSpec(memory_space=pltpu.SMEM)
    hbm = pl.BlockSpec(memory_space=pl.ANY)
    return pl.pallas_call(
        functools.partial(scan_kernel, micro, group_rows, slots, taps),
        in_specs=[smem, smem] + [vmem] * 4 + [hbm] * 6,
        out_specs=[vmem] * 2 + [hbm] * 3,
        out_shape=shapes,
        input_output_aliases={9: 2, 10: 3, 11: 4},
        scratch_shapes=[
            pltpu.VMEM((rows + 8, channels), F32),
            pltpu.VMEM((rows + 8, 2 * STATE), F32),
            pltpu.VMEM((rows, channels), BF),
            pltpu.VMEM((rows, channels), BF),
            pltpu.VMEM((rows, channels), BF),
            pltpu.VMEM(const.shape, F32),
            pltpu.VMEM(state.shape, F32),
            *[pltpu.VMEM(o.shape, o.dtype) for o in old],
            pltpu.VMEM((slots, channels, block), BF),
            pltpu.SemaphoreType.DMA((slots,)),
            pltpu.SemaphoreType.DMA((3,)),
        ],
        compiler_params=params(SCAN_MIB),
        cost_estimate=cost(2 * rows * channels * (rows + STATE + width), 2 * w_out.size),
    )(groups, flag, x_proj, here, over, dt_raw, *far)


def state_kernel(end_ref, weighted_ref, b_ref, state_ref, value_ref, out_ref, copy_ref):
    heads, dim, _ = state_ref.shape
    copy_ref[...] = value_ref[...]
    added = lax.dot_general(
        weighted_ref[...], b_ref[...], (((0,), (0,)), ((), ())), preferred_element_type=F32
    )
    for j in range(heads):
        out_ref[j] = end_ref[0, j] * state_ref[j] + added[j * dim:(j + 1) * dim, :]


def state_update(end, weighted, b_mat, state, value):
    vmem = pl.BlockSpec(memory_space=pltpu.VMEM)
    return pl.pallas_call(
        state_kernel,
        in_specs=[pl.BlockSpec(memory_space=pltpu.SMEM)] + [vmem] * 4,
        out_specs=[vmem, vmem],
        out_shape=[jax.ShapeDtypeStruct(state.shape, F32), jax.ShapeDtypeStruct(value.shape, value.dtype)],
        compiler_params=params(12),
        cost_estimate=cost(2 * weighted.size * b_mat.shape[1], 8 * state.size),
    )(end, weighted, b_mat, state, value)


def rms_rows(rows_in, gain):
    floats = rows_in.astype(F32)
    scaled = floats * lax.rsqrt(jnp.mean(floats * floats, axis=-1, keepdims=True) + 1e-05)
    return (scaled * gain[None, :]).astype(BF)


def per_device(hidden, norm_gain, w_x, w_bc, w_dt, conv_x, conv_bc, dt_bias, a_rate, d_skip, w_out,
               ssm_init, conv_x_init, conv_bc_init):
    segment = lax.axis_index("pipe")
    segments = lax.axis_size("pipe")
    head = lax.axis_index("head")
    devices = lax.axis_size("head")
    chips = devices // 2
    micro, local, width = hidden.shape
    own_rows = micro * local
    rows = own_rows * devices
    half = rows // 2
    local_heads = dt_bias.shape[1]
    channels = w_x.shape[2]
    bc_cols = w_bc.shape[2]
    span = bc_cols // GROUPS

    everyone = jnp.arange(devices)
    distance = (ring_place(head // 2, chips) - ring_place(everyone // 2, chips)) % chips
    place = ((everyone ^ head) % 2) * chips + distance
    groups = (place[None, :] * micro + jnp.arange(micro)[:, None]).reshape(-1)
    groups = jnp.concatenate([head[None], groups]).astype(jnp.int32)

    my_group = head * GROUPS // devices
    tail_bc = lax.dynamic_index_in_dim(conv_bc_init[0].reshape(-1, 2 * STATE, GROUPS), my_group, 2, keepdims=False)
    taps_bc = lax.dynamic_index_in_dim(conv_bc[0].reshape(-1, 2 * STATE, GROUPS), my_group, 2, keepdims=False)
    skip = jnp.repeat(d_skip[0], channels // local_heads)[None, :]

    taps = conv_x.shape[1]
    const_cols = max(channels, 2 * STATE)

    def wide(values):
        return jnp.pad(values, ((0, 0), (0, const_cols - values.shape[1])))

    const = jnp.concatenate([
        wide(a) for a in (conv_x_init[0], conv_x[0], skip, tail_bc, taps_bc, dt_bias, a_rate)
    ])
    const = jnp.pad(const, ((0, -const.shape[0] % 8), (0, 0)))

    block = 256 if channels >= 2048 else 128
    count = channels // block
    kept = min(HELD, count - 1)
    in_sum = min(SUM_LOADS, kept)
    inner_plan = [(w_x[0], block, i) for i in range(kept)]
    go = groups

    current = hidden.reshape(own_rows, width)
    out_rows = jnp.zeros((own_rows, width), BF)
    old = (
        jnp.zeros((rows, channels), BF),
        jnp.zeros((rows, STATE), BF),
        jnp.zeros((1, local_heads), F32),
    )
    held = []
    for tick in range(segments):
        last = tick + 1 == segments
        active = segment == tick
        flag = active.astype(jnp.int32).reshape(1)
        normed = rms_rows(current, norm_gain[0])
        arrived = [ring_shift(normed, s) for s in range(1, chips)]
        if tick:
            more, normed = load_beside(go, inner_plan[in_sum:], normed)
            held = held + more
        pieces = [normed] + arrived
        if own_rows % 16:
            pieces = [jnp.concatenate(pieces, axis=0)]
        pieces = pieces + [core_swap(piece) for piece in pieces]
        normed_all, dt_raw, bc_out = project_first(go, pieces, micro, local, w_bc[0], w_dt[0].T)
        bc_parts = [bc_out[:, s * 2 * span:(s + 1) * 2 * span] for s in range(chips)]
        bc_here = bc_parts[0]
        bc_parts = [ring_shift(bc_parts[s], s) for s in range(1, chips)]
        x_proj, bc_here = held_inner(go, normed_all, held, w_x[0], block, bc_here)
        bc_here = join([bc_here] + bc_parts)
        mine, other, *old = scan_and_out(
            micro, local, taps, groups, flag, x_proj, bc_here, core_swap(bc_here), dt_raw, const, ssm_init[0], old, w_out[0]
        )
        received = core_swap(other)
        pair = (mine.astype(F32) + received.astype(F32)).astype(BF)
        arrived = [ring_shift(pair[s * own_rows:(s + 1) * own_rows], s) for s in range(1, chips)]
        own = pair[:own_rows]
        if last:
            state_out, own = state_update(old[2], old[0], old[1], ssm_init[0], own)
        else:
            held, own = load_beside(go, inner_plan[:in_sum], own)
        total = own.astype(F32)
        for piece in arrived:
            total = total + piece.astype(F32)
        new_rows = (current.astype(F32) + total).astype(BF)
        out_rows = jnp.where(active, new_rows, out_rows)
        if not last:
            current = next_segment(new_rows, tick)
    return (out_rows.reshape(1, micro, local, width), state_out[None])


def solution(mesh):
    in_specs = (
        P(None, "head", None),
        P("pipe", None),
        P("pipe", None, "head"),
        P("pipe", None, "head"),
        P("pipe", None, "head"),
        P("pipe", None, "head"),
        P("pipe", None, None),
        P("pipe", "head"),
        P("pipe", "head"),
        P("pipe", "head"),
        P("pipe", "head", None),
        P("pipe", "head", None, None),
        P("pipe", None, "head"),
        P("pipe", None, None),
    )
    out_specs = (P("pipe", None, "head", None), P("pipe", "head", None, None))
    return jax.shard_map(
        per_device, mesh=mesh, in_specs=in_specs, out_specs=out_specs, check_vma=False
    )
```

```python
import functools

import jax
import jax.numpy as jnp
from jax import lax
from jax.experimental import pallas as pl
from jax.experimental.pallas import tpu as pltpu
from jax.sharding import PartitionSpec as P

STATE = 256
GROUPS = 8
MIB = 1 << 20
BF = jnp.bfloat16
F32 = jnp.float32
HIGHEST = lax.Precision.HIGHEST
SUM_LOADS = 5
HELD = 8
SLOTS = 4
BC_HELD = True
OUT_COLS = 1024
SCAN_MIB = 28


def whole(shape):
    return pl.BlockSpec(shape, lambda *_: (0,) * len(shape))


def cost(flops, nbytes):
    return pl.CostEstimate(flops=int(flops), bytes_accessed=int(nbytes), transcendentals=0)


def params(mib):
    return pltpu.CompilerParams(vmem_limit_bytes=mib * MIB)


def dot(a, b, **kw):
    return jnp.dot(a, b, preferred_element_type=F32, **kw)


def ring_place(chip, chips):
    return chip ^ (chip >> 1) if chips == 4 else chip


def core_swap(value):
    count = lax.axis_size("head")
    return lax.ppermute(value, "head", [(i, i ^ 1) for i in range(count)])


def ring_shift(value, steps):
    chips = lax.axis_size("head") // 2
    ring = [ring_place(i, chips) for i in range(chips)]
    pairs = [
        (2 * ring[i] + c, 2 * ring[(i + steps) % chips] + c) for i in range(chips) for c in range(2)
    ]
    return lax.ppermute(value, "head", pairs)


def next_segment(value, tick):
    count = lax.axis_size("pipe")
    pairs = []
    for low in range(tick % 2, count - 1, 2):
        pairs += [(low, low + 1), (low + 1, low)]
    return lax.ppermute(value, "pipe", pairs)


def bits(value, low, size):
    return (value >> (low.bit_length() - 1)) & (size - 1)


def iotas(rows, cols):
    return (
        lax.broadcasted_iota(jnp.int32, (rows, 1), 0),
        lax.broadcasted_iota(jnp.int32, (1, cols), 1),
    )


def device_at(head, distance, core, chips):
    place = (ring_place(head >> 1, chips) + distance) & (chips - 1)
    return 2 * ring_place(place, chips) + ((head & 1) ^ core)


def gather_order(head, rows, micro, local):
    devices = rows // (micro * local)
    chips = devices // 2
    time, place = iotas(rows, rows)
    device, block = bits(time, local, devices), bits(time, local * devices, micro)
    distance = (ring_place(head >> 1, chips) - ring_place(device >> 1, chips)) & (chips - 1)
    core = (device ^ head) & 1
    at = (((core * chips + distance) * micro) + block) * local + bits(time, 1, local)
    return (at == place).astype(F32).astype(BF)


def scatter_order(head, rows, micro, local):
    devices = rows // (micro * local)
    chips = devices // 2
    place, time = iotas(rows, rows)
    own = micro * local
    device = device_at(head, bits(place, own, chips), bits(place, own * chips, 2), chips)
    at = bits(place, local, micro) * (local * devices) + device * local + bits(place, 1, local)
    return (at == time).astype(F32).astype(BF)


def pick_columns(head, first, count, bc_cols, devices):
    chips, span = devices // 2, bc_cols // GROUPS
    column, sent = iotas(count, 2 * span * chips)
    device = device_at(head, bits(sent, 2 * span, chips), bits(sent, span, 2), chips)
    group = (device * GROUPS) >> (devices.bit_length() - 1)
    return (bits(sent, 1, span) * GROUPS + group == column + first).astype(F32).astype(BF)


def place_columns(head, core, devices):
    chips, span = devices // 2, 2 * STATE // devices
    sent, column = iotas(2 * STATE, 2 * STATE)
    device = device_at(head, -bits(sent, 2 * span, chips), core, chips)
    here = jnp.where(bits(sent, span, 2) == core, device * span + bits(sent, 1, span), -1)
    return (here == column).astype(F32).astype(BF)


def load_kernel(plan, go_ref, *refs):
    weights = max(p[0] for p in plan) + 1
    count = len(plan)
    sources, value_ref = refs[:weights], refs[weights]
    held, copy_ref, sems = refs[weights + 1:-2], refs[-2], refs[-1]
    copies = []
    for i, (which, index) in enumerate(plan):
        cols = held[i].shape[1]
        copies.append(
            pltpu.make_async_copy(sources[which].at[:, pl.ds(index * cols, cols)], held[i], sems.at[i])
        )
        copies[-1].start()

    @pl.when(go_ref[0] >= 0)
    def _():
        copy_ref[...] = value_ref[...]

    for i in range(count):
        copies[i].wait()


def load_beside(go, plan, value):
    if not plan:
        return [], value
    weights = []
    for weight, _, _ in plan:
        if not any(weight is w for w in weights):
            weights.append(weight)
    steps = [([weight is w for w in weights].index(True), index) for weight, _, index in plan]
    vmem = pl.BlockSpec(memory_space=pltpu.VMEM)
    nbytes = sum(2 * w.shape[0] * cols for w, cols, _ in plan)
    *held, value = pl.pallas_call(
        functools.partial(load_kernel, steps),
        in_specs=[pl.BlockSpec(memory_space=pltpu.SMEM)] + [pl.BlockSpec(memory_space=pl.ANY)] * len(weights) + [vmem],
        out_specs=[vmem] * (len(plan) + 1),
        out_shape=[pltpu.VMEM((w.shape[0], cols), w.dtype) for w, cols, _ in plan]
        + [jax.ShapeDtypeStruct(value.shape, value.dtype)],
        scratch_shapes=[pltpu.SemaphoreType.DMA((len(plan),))],
        compiler_params=params(2),
        cost_estimate=cost(0, nbytes),
    )(go, *[pltpu.with_memory_space_constraint(w, pltpu.HBM) for w in weights], value)
    return held, value


def first_kernel(count, held_count, micro, local, *refs):
    pieces, go_ref, wdt_ref, wbc_ref = refs[:count], *refs[count:count + 3]
    held, (normed_ref, dt_ref, bc_ref, late, wdt, sems) = refs[count + 3:count + 3 + held_count], refs[count + 3 + held_count:]
    rows = pieces[0].shape[0]
    bc_cols = wbc_ref.shape[1]
    cols = held[0].shape[1] if held else late.shape[2]
    blocks = bc_cols // cols

    def fetch(i):
        return pltpu.make_async_copy(wbc_ref.at[:, pl.ds(i * cols, cols)], late.at[i], sems.at[i])

    steps = pltpu.make_async_copy(wdt_ref, wdt, sems.at[sems.shape[0] - 1])
    steps.start()
    if not held:
        for i in range(blocks):
            fetch(i).start()

    @pl.when(go_ref[0] >= 0)
    def _():
        for i, piece in enumerate(pieces):
            normed_ref[i * rows:(i + 1) * rows, :] = piece[...]

    steps.wait()
    dt_ref[...] = lax.dot_general(
        normed_ref[...], wdt[...], (((1,), (1,)), ((), ())), preferred_element_type=F32
    )
    head = go_ref[0]
    all_rows = normed_ref.shape[0]
    devices = all_rows // (micro * local)
    gather = gather_order(head, all_rows, micro, local)
    total = jnp.zeros(bc_ref.shape, F32)
    for i in range(blocks):
        if not held:
            fetch(i).wait()
        part = dot(normed_ref[...], held[i][...] if held else late[i]).astype(BF)
        part = dot(gather, part).astype(BF)
        total += dot(part, pick_columns(head, i * cols, cols, blocks * cols, devices))
    bc_ref[...] = total.astype(BF)


def project_first(go, pieces, micro, local, w_bc, w_dt, held):
    width, bc_cols = w_bc.shape
    rows = len(pieces) * pieces[0].shape[0]
    heads = w_dt.shape[0]
    vmem = pl.BlockSpec(memory_space=pltpu.VMEM)
    block = min(256, bc_cols)
    args = (*pieces, go, pltpu.with_memory_space_constraint(w_dt, pltpu.HBM), pltpu.with_memory_space_constraint(w_bc, pltpu.HBM))
    args += tuple(pltpu.with_memory_space_constraint(w, pltpu.VMEM) for w in held)
    late = (1, 16, 128) if held else (bc_cols // block, width, block)
    shapes = [
        jax.ShapeDtypeStruct((rows, width), BF),
        jax.ShapeDtypeStruct((rows, heads), F32),
        jax.ShapeDtypeStruct((rows, bc_cols // GROUPS * (rows // (micro * local))), BF),
    ]
    return pl.pallas_call(
        functools.partial(first_kernel, len(pieces), len(held), micro, local),
        in_specs=[vmem] * len(pieces) + [pl.BlockSpec(memory_space=pltpu.SMEM)]
        + [pl.BlockSpec(memory_space=pl.ANY)] * 2 + [vmem] * len(held),
        out_specs=[vmem] * 3,
        out_shape=shapes,
        scratch_shapes=[
            pltpu.VMEM(late, BF),
            pltpu.VMEM(w_dt.shape, BF),
            pltpu.SemaphoreType.DMA((late[0] + 1,)),
        ],
        compiler_params=params(4 if held else 12),
        cost_estimate=cost(2 * rows * width * (bc_cols + heads), 2 * w_bc.size),
    )(*args)


def held_kernel(count, go_ref, normed_ref, value_ref, *refs):
    held, (w_ref, x_ref, copy_ref, late, sems) = refs[:count], refs[count:]
    cols = late.shape[2]
    rest = w_ref.shape[1] // cols - count

    def fetch(i):
        return pltpu.make_async_copy(w_ref.at[:, pl.ds((count + i) * cols, cols)], late.at[i], sems.at[i])

    for i in range(rest):
        fetch(i).start()

    @pl.when(go_ref[0] >= 0)
    def _():
        copy_ref[...] = value_ref[...]
        for i, block_ref in enumerate(held):
            x_ref[:, i * cols:(i + 1) * cols] = dot(normed_ref[...], block_ref[...])

    for i in range(rest):
        fetch(i).wait()
        x_ref[:, (count + i) * cols:(count + i + 1) * cols] = dot(normed_ref[...], late[i])


def held_inner(go, normed, held, weight, block, value):
    rows, width = normed.shape
    cols = weight.shape[1]
    rest = cols // block - len(held)
    vmem = pl.BlockSpec(memory_space=pltpu.VMEM)
    return pl.pallas_call(
        functools.partial(held_kernel, len(held)),
        in_specs=[pl.BlockSpec(memory_space=pltpu.SMEM)] + [vmem] * (len(held) + 2) + [pl.BlockSpec(memory_space=pl.ANY)],
        out_specs=[vmem, vmem],
        out_shape=[jax.ShapeDtypeStruct((rows, cols), F32), jax.ShapeDtypeStruct(value.shape, value.dtype)],
        scratch_shapes=[
            pltpu.VMEM((rest, width, block) if rest else (1, 16, block), BF),
            pltpu.SemaphoreType.DMA((max(rest, 1),)),
        ],
        compiler_params=params(4 + 2 * rest * width * block // MIB),
        cost_estimate=cost(2 * rows * width * cols, 2 * rows * width),
    )(go, normed, value, *[pltpu.with_memory_space_constraint(w, pltpu.VMEM) for w in held],
      pltpu.with_memory_space_constraint(weight, pltpu.HBM))


def join_kernel(*refs):
    lanes = refs[0].shape[1]
    for i, ref in enumerate(refs[:-1]):
        refs[-1][:, i * lanes:(i + 1) * lanes] = ref[...]


def join(parts):
    rows, lanes = parts[0].shape
    if lanes % 128:
        return jnp.concatenate(parts, axis=1)
    vmem = pl.BlockSpec(memory_space=pltpu.VMEM)
    return pl.pallas_call(
        join_kernel,
        in_specs=[vmem] * len(parts),
        out_specs=vmem,
        out_shape=jax.ShapeDtypeStruct((rows, lanes * len(parts)), parts[0].dtype),
        compiler_params=params(1),
        cost_estimate=cost(0, 4 * rows * lanes * len(parts)),
    )(*parts)


def conv_silu(pad_ref, const_ref, first, taps):
    rows, cols = pad_ref.shape[0] - 8, pad_ref.shape[1]
    pad_ref[8 - (taps - 1):8, :] = const_ref[first:first + taps - 1, :cols]
    at = first + taps - 1
    total = const_ref[at:at + 1, :cols] * pad_ref[pl.ds(9 - taps, rows), :]
    for k in range(1, taps):
        total = total + const_ref[at + k:at + k + 1, :cols] * pad_ref[pl.ds(9 - taps + k, rows), :]
    return total * jax.nn.sigmoid(total)


def in_time(order, groups_ref, group_rows, src_ref, dst_ref):
    rows = src_ref.shape[0]
    if group_rows % 8:
        dst_ref[8:, :] = dot(order.astype(F32), src_ref[...], precision=HIGHEST)
        return
    for g in range(rows // group_rows):
        start = pl.multiple_of(groups_ref[1 + g] * group_rows, group_rows)
        dst_ref[8 + g * group_rows:8 + (g + 1) * group_rows, :] = src_ref[pl.ds(start, group_rows), :]


def spread_exact(values, spread):
    high = values.astype(BF)
    rest = values - high.astype(F32)
    mid = rest.astype(BF)
    low = (rest - mid.astype(F32)).astype(BF)
    return dot(jnp.concatenate([high, mid, low], axis=1), spread)


def scan_kernel(micro, group_rows, slots, taps, groups_ref, flag_ref, x_ref, here_ref, over_ref, dt_ref, const_ref, state_ref,
                w_ref, _weighted, _b, _end, own_ref, other_ref, weighted_ref, b_ref, end_ref, pad_x, pad_bc, scaled, y_ref,
                sorted_ref, const, state_buf, weighted_buf, b_buf, end_buf, ring, sems, own_sems):
    pieces = (own_ref, other_ref)
    count = 0
    rows, channels = y_ref.shape
    active = flag_ref[0] == 1
    heads = dt_ref.shape[1]
    dim = channels // heads
    half = STATE
    devices = rows // (micro * group_rows)
    head = groups_ref[0]
    block = ring.shape[2]
    blocks = w_ref.shape[1] // block

    def fetch(i):
        slot = lax.rem(i, slots)
        cols = pl.ds(pl.multiple_of(i * block, block), block)
        return pltpu.make_async_copy(w_ref.at[:, cols], ring.at[slot], sems.at[slot])

    loads = [pltpu.make_async_copy(const_ref, const, own_sems.at[0]), pltpu.make_async_copy(state_ref, state_buf, own_sems.at[1])]
    for copy in loads:
        copy.start()
    for i in range(min(slots, blocks)):
        fetch(i).start()

    @pl.when(groups_ref[0] >= 0)
    def _():
        arrived = dot(here_ref[...], place_columns(head, 0, devices)) + dot(over_ref[...], place_columns(head, 1, devices))
        pad_bc[8:, :] = arrived
        gather = gather_order(head, rows, micro, group_rows)
        loads[0].wait()
        bc = conv_silu(pad_bc, const, 2 * taps, taps)
        b_mat, c_mat = bc[:, :half], bc[:, half:]
        b_bf, c_bf = b_mat.astype(BF), c_mat.astype(BF)
        b_buf[...] = b_bf
        contract = (((1,), (1,)), ((), ()))
        scores = lax.dot_general(c_mat, b_mat, contract, precision=HIGHEST, preferred_element_type=F32)
        t_ids = lax.broadcasted_iota(jnp.int32, (rows, rows), 0)
        s_ids = lax.broadcasted_iota(jnp.int32, (rows, rows), 1)
        causal = t_ids >= s_ids
        scores = jnp.where(causal, scores, 0.0)

        raw = dot(gather.astype(F32), dt_ref[...], precision=HIGHEST) + const[4 * taps - 1:4 * taps, :heads]
        step = jnp.maximum(raw, 0.0) + jnp.log1p(jnp.exp(-jnp.abs(raw)))
        log_decay = dot(causal.astype(F32), -step * const[4 * taps:4 * taps + 1, :heads], precision=HIGHEST)
        end_log = log_decay[rows - 1:rows, :]
        end_buf[...] = jnp.exp(end_log)
        part_head, channel = iotas(3 * heads, channels)
        spread = (bits(part_head, 1, heads) == (channel >> (dim.bit_length() - 1))).astype(F32).astype(BF)
        step_full = spread_exact(step, spread)
        to_end_full = spread_exact(jnp.exp(end_log - log_decay), spread)
        decay_full = spread_exact(jnp.exp(log_decay), spread)
        log_rows = log_decay.T

        in_time(gather, groups_ref, group_rows, x_ref, pad_x)
        x_conv = conv_silu(pad_x, const, 0, taps)
        stepped = x_conv * step_full
        scaled[...] = stepped.astype(BF)
        weighted_buf[...] = (stepped * to_end_full).astype(BF)
        for j in range(heads):
            gap = jnp.minimum(log_decay[:, j:j + 1] - log_rows[j:j + 1, :], 0.0)
            weight = (scores * jnp.exp(gap)).astype(BF)
            cols = slice(j * dim, (j + 1) * dim)
            pad_x[8:, cols] = const[2 * taps - 1:2 * taps, cols] * x_conv[:, cols] + dot(weight, scaled[:, cols])

        loads[1].wait()
        state = state_buf[...].reshape(channels, half).astype(BF)
        carried = lax.dot_general(c_bf, state, contract, preferred_element_type=F32)
        y_ref[...] = (pad_x[8:, :] + carried * decay_full).astype(BF)

    kept = [
        pltpu.make_async_copy(src, dst, own_sems.at[i])
        for i, (src, dst) in enumerate(((weighted_buf, weighted_ref), (b_buf, b_ref), (end_buf, end_ref)))
    ]

    @pl.when(active)
    def _():
        for copy in kept:
            copy.start()

    sorted_ref[...] = dot(scatter_order(head, rows, micro, group_rows), y_ref[...]).astype(BF)
    size = rows // 2

    @pl.loop(0, blocks)
    def _(i):
        fetch(i).wait()
        part = dot(sorted_ref[...], ring[lax.rem(i, slots)]).astype(BF)
        cols = pl.ds(pl.multiple_of(i * block, block), block)
        for q, piece in enumerate(pieces):
            piece[:, cols] = part[q * size:(q + 1) * size, :]

        @pl.when(i + slots < blocks)
        def _():
            fetch(i + slots).start()

    @pl.when(active)
    def _():
        for copy in kept:
            copy.wait()


def scan_and_out(micro, group_rows, taps, groups, flag, x_proj, here, over, dt_raw, const, state, old, w_out):
    rows, channels = x_proj.shape
    width = w_out.shape[1]
    block, slots = OUT_COLS, SLOTS
    far = [pltpu.with_memory_space_constraint(a, pltpu.HBM) for a in (const, state, w_out, *old)]
    shapes = [jax.ShapeDtypeStruct((rows // 2, width), BF)] * 2 + [jax.ShapeDtypeStruct(o.shape, o.dtype) for o in old]
    vmem = pl.BlockSpec(memory_space=pltpu.VMEM)
    smem = pl.BlockSpec(memory_space=pltpu.SMEM)
    hbm = pl.BlockSpec(memory_space=pl.ANY)
    return pl.pallas_call(
        functools.partial(scan_kernel, micro, group_rows, slots, taps),
        in_specs=[smem, smem] + [vmem] * 4 + [hbm] * 6,
        out_specs=[vmem] * 2 + [hbm] * 3,
        out_shape=shapes,
        input_output_aliases={9: 2, 10: 3, 11: 4},
        scratch_shapes=[
            pltpu.VMEM((rows + 8, channels), F32),
            pltpu.VMEM((rows + 8, 2 * STATE), F32),
            pltpu.VMEM((rows, channels), BF),
            pltpu.VMEM((rows, channels), BF),
            pltpu.VMEM((rows, channels), BF),
            pltpu.VMEM(const.shape, F32),
            pltpu.VMEM(state.shape, F32),
            *[pltpu.VMEM(o.shape, o.dtype) for o in old],
            pltpu.VMEM((slots, channels, block), BF),
            pltpu.SemaphoreType.DMA((slots,)),
            pltpu.SemaphoreType.DMA((3,)),
        ],
        compiler_params=params(SCAN_MIB),
        cost_estimate=cost(2 * rows * channels * (rows + STATE + width), 2 * w_out.size),
    )(groups, flag, x_proj, here, over, dt_raw, *far)


def state_kernel(end_ref, weighted_ref, b_ref, state_ref, value_ref, out_ref, copy_ref):
    heads, dim, _ = state_ref.shape
    copy_ref[...] = value_ref[...]
    added = lax.dot_general(
        weighted_ref[...], b_ref[...], (((0,), (0,)), ((), ())), preferred_element_type=F32
    )
    for j in range(heads):
        out_ref[j] = end_ref[0, j] * state_ref[j] + added[j * dim:(j + 1) * dim, :]


def state_update(end, weighted, b_mat, state, value):
    vmem = pl.BlockSpec(memory_space=pltpu.VMEM)
    return pl.pallas_call(
        state_kernel,
        in_specs=[pl.BlockSpec(memory_space=pltpu.SMEM)] + [vmem] * 4,
        out_specs=[vmem, vmem],
        out_shape=[jax.ShapeDtypeStruct(state.shape, F32), jax.ShapeDtypeStruct(value.shape, value.dtype)],
        compiler_params=params(12),
        cost_estimate=cost(2 * weighted.size * b_mat.shape[1], 8 * state.size),
    )(end, weighted, b_mat, state, value)


def rms_rows(rows_in, gain):
    floats = rows_in.astype(F32)
    scaled = floats * lax.rsqrt(jnp.mean(floats * floats, axis=-1, keepdims=True) + 1e-05)
    return (scaled * gain[None, :]).astype(BF)


def per_device(hidden, norm_gain, w_x, w_bc, w_dt, conv_x, conv_bc, dt_bias, a_rate, d_skip, w_out,
               ssm_init, conv_x_init, conv_bc_init):
    segment = lax.axis_index("pipe")
    segments = lax.axis_size("pipe")
    head = lax.axis_index("head")
    devices = lax.axis_size("head")
    chips = devices // 2
    micro, local, width = hidden.shape
    own_rows = micro * local
    rows = own_rows * devices
    half = rows // 2
    local_heads = dt_bias.shape[1]
    channels = w_x.shape[2]
    bc_cols = w_bc.shape[2]
    span = bc_cols // GROUPS

    everyone = jnp.arange(devices)
    distance = (ring_place(head // 2, chips) - ring_place(everyone // 2, chips)) % chips
    place = ((everyone ^ head) % 2) * chips + distance
    groups = (place[None, :] * micro + jnp.arange(micro)[:, None]).reshape(-1)
    groups = jnp.concatenate([head[None], groups]).astype(jnp.int32)

    my_group = head * GROUPS // devices
    tail_bc = lax.dynamic_index_in_dim(conv_bc_init[0].reshape(-1, 2 * STATE, GROUPS), my_group, 2, keepdims=False)
    taps_bc = lax.dynamic_index_in_dim(conv_bc[0].reshape(-1, 2 * STATE, GROUPS), my_group, 2, keepdims=False)
    skip = jnp.repeat(d_skip[0], channels // local_heads)[None, :]

    taps = conv_x.shape[1]
    const_cols = max(channels, 2 * STATE)

    def wide(values):
        return jnp.pad(values, ((0, 0), (0, const_cols - values.shape[1])))

    const = jnp.concatenate([
        wide(a) for a in (conv_x_init[0], conv_x[0], skip, tail_bc, taps_bc, dt_bias, a_rate)
    ])
    const = jnp.pad(const, ((0, -const.shape[0] % 8), (0, 0)))

    block = 256 if channels >= 2048 else 128
    count = channels // block
    kept = min(HELD, count)
    in_sum = min(SUM_LOADS, kept)
    inner_plan = [(w_x[0], block, i) for i in range(kept)]
    go = groups

    current = hidden.reshape(own_rows, width)
    out_rows = jnp.zeros((own_rows, width), BF)
    old = (
        jnp.zeros((rows, channels), BF),
        jnp.zeros((rows, STATE), BF),
        jnp.zeros((1, local_heads), F32),
    )
    bc_plan = [(w_bc[0], 256, i) for i in range(bc_cols // 256)] if BC_HELD else []
    held, held_bc = [], []
    for tick in range(segments):
        last = tick + 1 == segments
        active = segment == tick
        flag = active.astype(jnp.int32).reshape(1)
        normed = rms_rows(current, norm_gain[0])
        arrived = [ring_shift(normed, s) for s in range(1, chips)]
        if tick:
            more, normed = load_beside(go, inner_plan[in_sum:] + bc_plan, normed)
            held, held_bc = held + more[:kept - in_sum], more[kept - in_sum:]
        pieces = [normed] + arrived
        if own_rows % 16:
            pieces = [jnp.concatenate(pieces, axis=0)]
        pieces = pieces + [core_swap(piece) for piece in pieces]
        normed_all, dt_raw, bc_out = project_first(go, pieces, micro, local, w_bc[0], w_dt[0].T, held_bc)
        bc_parts = [bc_out[:, s * 2 * span:(s + 1) * 2 * span] for s in range(chips)]
        bc_here = bc_parts[0]
        bc_parts = [ring_shift(bc_parts[s], s) for s in range(1, chips)]
        x_proj, bc_here = held_inner(go, normed_all, held, w_x[0], block, bc_here)
        bc_here = join([bc_here] + bc_parts)
        mine, other, *old = scan_and_out(
            micro, local, taps, groups, flag, x_proj, bc_here, core_swap(bc_here), dt_raw, const, ssm_init[0], old, w_out[0]
        )
        received = core_swap(other)
        pair = (mine.astype(F32) + received.astype(F32)).astype(BF)
        arrived = [ring_shift(pair[s * own_rows:(s + 1) * own_rows], s) for s in range(1, chips)]
        own = pair[:own_rows]
        if last:
            state_out, own = state_update(old[2], old[0], old[1], ssm_init[0], own)
        else:
            held, own = load_beside(go, inner_plan[:in_sum], own)
        total = own.astype(F32)
        for piece in arrived:
            total = total + piece.astype(F32)
        new_rows = (current.astype(F32) + total).astype(BF)
        out_rows = jnp.where(active, new_rows, out_rows)
        if not last:
            current = next_segment(new_rows, tick)
    return (out_rows.reshape(1, micro, local, width), state_out[None])


def solution(mesh):
    in_specs = (
        P(None, "head", None),
        P("pipe", None),
        P("pipe", None, "head"),
        P("pipe", None, "head"),
        P("pipe", None, "head"),
        P("pipe", None, "head"),
        P("pipe", None, None),
        P("pipe", "head"),
        P("pipe", "head"),
        P("pipe", "head"),
        P("pipe", "head", None),
        P("pipe", "head", None, None),
        P("pipe", None, "head"),
        P("pipe", None, None),
    )
    out_specs = (P("pipe", None, "head", None), P("pipe", "head", None, None))
    return jax.shard_map(
        per_device, mesh=mesh, in_specs=in_specs, out_specs=out_specs, check_vma=False
    )
```

```python
import functools

import jax
import jax.numpy as jnp
from jax import lax
from jax.experimental import pallas as pl
from jax.experimental.pallas import tpu as pltpu
from jax.sharding import PartitionSpec as P

STATE = 256
GROUPS = 8
MIB = 1 << 20
BF = jnp.bfloat16
F32 = jnp.float32
HIGHEST = lax.Precision.HIGHEST
SUM_LOADS = 5
HELD = 8
SLOTS = 4
BC_HELD = True
OUT_COLS = 1024
SCAN_MIB = 28


def whole(shape):
    return pl.BlockSpec(shape, lambda *_: (0,) * len(shape))


def cost(flops, nbytes):
    return pl.CostEstimate(flops=int(flops), bytes_accessed=int(nbytes), transcendentals=0)


def params(mib):
    return pltpu.CompilerParams(vmem_limit_bytes=mib * MIB)


def dot(a, b, **kw):
    return jnp.dot(a, b, preferred_element_type=F32, **kw)


def ring_place(chip, chips):
    return chip ^ (chip >> 1) if chips == 4 else chip


def core_swap(value):
    count = lax.axis_size("head")
    return lax.ppermute(value, "head", [(i, i ^ 1) for i in range(count)])


def ring_shift(value, steps):
    chips = lax.axis_size("head") // 2
    ring = [ring_place(i, chips) for i in range(chips)]
    pairs = [
        (2 * ring[i] + c, 2 * ring[(i + steps) % chips] + c) for i in range(chips) for c in range(2)
    ]
    return lax.ppermute(value, "head", pairs)


def next_segment(value, tick):
    count = lax.axis_size("pipe")
    pairs = []
    for low in range(tick % 2, count - 1, 2):
        pairs += [(low, low + 1), (low + 1, low)]
    return lax.ppermute(value, "pipe", pairs)


def bits(value, low, size):
    return (value >> (low.bit_length() - 1)) & (size - 1)


def iotas(rows, cols):
    return (
        lax.broadcasted_iota(jnp.int32, (rows, 1), 0),
        lax.broadcasted_iota(jnp.int32, (1, cols), 1),
    )


def device_at(head, distance, core, chips):
    place = (ring_place(head >> 1, chips) + distance) & (chips - 1)
    return 2 * ring_place(place, chips) + ((head & 1) ^ core)


def gather_order(head, rows, micro, local):
    devices = rows // (micro * local)
    chips = devices // 2
    time, place = iotas(rows, rows)
    device, block = bits(time, local, devices), bits(time, local * devices, micro)
    distance = (ring_place(head >> 1, chips) - ring_place(device >> 1, chips)) & (chips - 1)
    core = (device ^ head) & 1
    at = (((core * chips + distance) * micro) + block) * local + bits(time, 1, local)
    return (at == place).astype(F32).astype(BF)


def scatter_order(head, rows, micro, local):
    devices = rows // (micro * local)
    chips = devices // 2
    place, time = iotas(rows, rows)
    own = micro * local
    device = device_at(head, bits(place, own, chips), bits(place, own * chips, 2), chips)
    at = bits(place, local, micro) * (local * devices) + device * local + bits(place, 1, local)
    return (at == time).astype(F32).astype(BF)


def pick_columns(head, first, count, bc_cols, devices):
    chips, span = devices // 2, bc_cols // GROUPS
    column, sent = iotas(count, 2 * span * chips)
    device = device_at(head, bits(sent, 2 * span, chips), bits(sent, span, 2), chips)
    group = (device * GROUPS) >> (devices.bit_length() - 1)
    return (bits(sent, 1, span) * GROUPS + group == column + first).astype(F32).astype(BF)


def place_columns(head, core, devices):
    chips, span = devices // 2, 2 * STATE // devices
    sent, column = iotas(2 * STATE, 2 * STATE)
    device = device_at(head, -bits(sent, 2 * span, chips), core, chips)
    here = jnp.where(bits(sent, span, 2) == core, device * span + bits(sent, 1, span), -1)
    return (here == column).astype(F32).astype(BF)


def load_kernel(plan, go_ref, *refs):
    weights = max(p[0] for p in plan) + 1
    count = len(plan)
    sources, value_ref = refs[:weights], refs[weights]
    held, copy_ref, sems = refs[weights + 1:-2], refs[-2], refs[-1]
    copies = []
    for i, (which, index) in enumerate(plan):
        cols = held[i].shape[1]
        copies.append(
            pltpu.make_async_copy(sources[which].at[:, pl.ds(index * cols, cols)], held[i], sems.at[i])
        )
        copies[-1].start()

    @pl.when(go_ref[0] >= 0)
    def _():
        copy_ref[...] = value_ref[...]

    for i in range(count):
        copies[i].wait()


def load_beside(go, plan, value):
    if not plan:
        return [], value
    weights = []
    for weight, _, _ in plan:
        if not any(weight is w for w in weights):
            weights.append(weight)
    steps = [([weight is w for w in weights].index(True), index) for weight, _, index in plan]
    vmem = pl.BlockSpec(memory_space=pltpu.VMEM)
    nbytes = sum(2 * w.shape[0] * cols for w, cols, _ in plan)
    *held, value = pl.pallas_call(
        functools.partial(load_kernel, steps),
        in_specs=[pl.BlockSpec(memory_space=pltpu.SMEM)] + [pl.BlockSpec(memory_space=pl.ANY)] * len(weights) + [vmem],
        out_specs=[vmem] * (len(plan) + 1),
        out_shape=[pltpu.VMEM((w.shape[0], cols), w.dtype) for w, cols, _ in plan]
        + [jax.ShapeDtypeStruct(value.shape, value.dtype)],
        scratch_shapes=[pltpu.SemaphoreType.DMA((len(plan),))],
        compiler_params=params(2),
        cost_estimate=cost(0, nbytes),
    )(go, *[pltpu.with_memory_space_constraint(w, pltpu.HBM) for w in weights], value)
    return held, value


def first_kernel(count, held_count, micro, local, *refs):
    pieces, go_ref, wdt_ref, wbc_ref = refs[:count], *refs[count:count + 3]
    held, (normed_ref, dt_ref, bc_ref, late, wdt, sems) = refs[count + 3:count + 3 + held_count], refs[-6:]
    rows = pieces[0].shape[0]
    bc_cols = wbc_ref.shape[1]
    cols = held[0].shape[1] if held else late.shape[2]
    blocks = bc_cols // cols

    def fetch(i):
        return pltpu.make_async_copy(wbc_ref.at[:, pl.ds(i * cols, cols)], late.at[i], sems.at[i])

    steps = pltpu.make_async_copy(wdt_ref, wdt, sems.at[sems.shape[0] - 1])
    steps.start()
    if not held:
        for i in range(blocks):
            fetch(i).start()

    @pl.when(go_ref[0] >= 0)
    def _():
        for i, piece in enumerate(pieces):
            normed_ref[i * rows:(i + 1) * rows, :] = piece[...]

    steps.wait()
    dt_ref[...] = lax.dot_general(
        normed_ref[...], wdt[...], (((1,), (1,)), ((), ())), preferred_element_type=F32
    )
    head = go_ref[0]
    all_rows = normed_ref.shape[0]
    devices = all_rows // (micro * local)
    gather = gather_order(head, all_rows, micro, local)
    total = jnp.zeros(bc_ref.shape, F32)
    for i in range(blocks):
        if not held:
            fetch(i).wait()
        part = dot(normed_ref[...], held[i][...] if held else late[i]).astype(BF)
        part = dot(gather, part).astype(BF)
        total += dot(part, pick_columns(head, i * cols, cols, blocks * cols, devices))
    bc_ref[...] = total.astype(BF)


def project_first(go, pieces, micro, local, w_bc, w_dt, held, ready):
    width, bc_cols = w_bc.shape
    rows = len(pieces) * pieces[0].shape[0]
    heads = w_dt.shape[0]
    vmem = pl.BlockSpec(memory_space=pltpu.VMEM)
    block = min(256, bc_cols)
    args = (*pieces, go, pltpu.with_memory_space_constraint(w_dt, pltpu.HBM), pltpu.with_memory_space_constraint(w_bc, pltpu.HBM))
    args += tuple(pltpu.with_memory_space_constraint(w, pltpu.VMEM) for w in held)
    args += tuple(pltpu.with_memory_space_constraint(a, pltpu.HBM) for a in ready)
    late = (1, 16, 128) if held else (bc_cols // block, width, block)
    shapes = [
        jax.ShapeDtypeStruct((rows, width), BF),
        jax.ShapeDtypeStruct((rows, heads), F32),
        jax.ShapeDtypeStruct((rows, bc_cols // GROUPS * (rows // (micro * local))), BF),
    ]
    return pl.pallas_call(
        functools.partial(first_kernel, len(pieces), len(held), micro, local),
        in_specs=[vmem] * len(pieces) + [pl.BlockSpec(memory_space=pltpu.SMEM)]
        + [pl.BlockSpec(memory_space=pl.ANY)] * 2 + [vmem] * len(held) + [pl.BlockSpec(memory_space=pl.ANY)] * len(ready),
        out_specs=[vmem] * 3,
        out_shape=shapes,
        scratch_shapes=[
            pltpu.VMEM(late, BF),
            pltpu.VMEM(w_dt.shape, BF),
            pltpu.SemaphoreType.DMA((late[0] + 1,)),
        ],
        compiler_params=params(4 if held else 12),
        cost_estimate=cost(2 * rows * width * (bc_cols + heads), 2 * w_bc.size),
    )(*args)


def held_kernel(count, go_ref, normed_ref, value_ref, *refs):
    held, (w_ref, x_ref, copy_ref, late, sems) = refs[:count], refs[count:]
    cols = late.shape[2]
    rest = w_ref.shape[1] // cols - count

    def fetch(i):
        return pltpu.make_async_copy(w_ref.at[:, pl.ds((count + i) * cols, cols)], late.at[i], sems.at[i])

    for i in range(rest):
        fetch(i).start()

    @pl.when(go_ref[0] >= 0)
    def _():
        copy_ref[...] = value_ref[...]
        for i, block_ref in enumerate(held):
            x_ref[:, i * cols:(i + 1) * cols] = dot(normed_ref[...], block_ref[...])

    for i in range(rest):
        fetch(i).wait()
        x_ref[:, (count + i) * cols:(count + i + 1) * cols] = dot(normed_ref[...], late[i])


def held_inner(go, normed, held, weight, block, value):
    rows, width = normed.shape
    cols = weight.shape[1]
    rest = cols // block - len(held)
    vmem = pl.BlockSpec(memory_space=pltpu.VMEM)
    return pl.pallas_call(
        functools.partial(held_kernel, len(held)),
        in_specs=[pl.BlockSpec(memory_space=pltpu.SMEM)] + [vmem] * (len(held) + 2) + [pl.BlockSpec(memory_space=pl.ANY)],
        out_specs=[vmem, vmem],
        out_shape=[jax.ShapeDtypeStruct((rows, cols), F32), jax.ShapeDtypeStruct(value.shape, value.dtype)],
        scratch_shapes=[
            pltpu.VMEM((rest, width, block) if rest else (1, 16, block), BF),
            pltpu.SemaphoreType.DMA((max(rest, 1),)),
        ],
        compiler_params=params(4 + 2 * rest * width * block // MIB),
        cost_estimate=cost(2 * rows * width * cols, 2 * rows * width),
    )(go, normed, value, *[pltpu.with_memory_space_constraint(w, pltpu.VMEM) for w in held],
      pltpu.with_memory_space_constraint(weight, pltpu.HBM))


def join_kernel(*refs):
    lanes = refs[0].shape[1]
    for i, ref in enumerate(refs[:-1]):
        refs[-1][:, i * lanes:(i + 1) * lanes] = ref[...]


def join(parts):
    rows, lanes = parts[0].shape
    if lanes % 128:
        return jnp.concatenate(parts, axis=1)
    vmem = pl.BlockSpec(memory_space=pltpu.VMEM)
    return pl.pallas_call(
        join_kernel,
        in_specs=[vmem] * len(parts),
        out_specs=vmem,
        out_shape=jax.ShapeDtypeStruct((rows, lanes * len(parts)), parts[0].dtype),
        compiler_params=params(1),
        cost_estimate=cost(0, 4 * rows * lanes * len(parts)),
    )(*parts)


def conv_silu(pad_ref, const_ref, first, taps):
    rows, cols = pad_ref.shape[0] - 8, pad_ref.shape[1]
    pad_ref[8 - (taps - 1):8, :] = const_ref[first:first + taps - 1, :cols]
    at = first + taps - 1
    total = const_ref[at:at + 1, :cols] * pad_ref[pl.ds(9 - taps, rows), :]
    for k in range(1, taps):
        total = total + const_ref[at + k:at + k + 1, :cols] * pad_ref[pl.ds(9 - taps + k, rows), :]
    return total * jax.nn.sigmoid(total)


def in_time(order, groups_ref, group_rows, src_ref, dst_ref):
    rows = src_ref.shape[0]
    if group_rows % 8:
        dst_ref[8:, :] = dot(order.astype(F32), src_ref[...], precision=HIGHEST)
        return
    for g in range(rows // group_rows):
        start = pl.multiple_of(groups_ref[1 + g] * group_rows, group_rows)
        dst_ref[8 + g * group_rows:8 + (g + 1) * group_rows, :] = src_ref[pl.ds(start, group_rows), :]


def spread_exact(values, spread):
    high = values.astype(BF)
    rest = values - high.astype(F32)
    mid = rest.astype(BF)
    low = (rest - mid.astype(F32)).astype(BF)
    return dot(jnp.concatenate([high, mid, low], axis=1), spread)


def scan_kernel(micro, group_rows, slots, taps, passed, *refs):
    scan_body(micro, group_rows, slots, taps, *refs[:9], *refs[9 + passed:])


def scan_body(micro, group_rows, slots, taps, groups_ref, flag_ref, x_ref, here_ref, over_ref, dt_ref, const_ref, state_ref,
                w_ref, own_ref, other_ref, weighted_ref, b_ref, end_ref, pad_x, pad_bc, scaled, y_ref,
                sorted_ref, const, state_buf, weighted_buf, b_buf, end_buf, ring, sems, own_sems):
    pieces = (own_ref, other_ref)
    count = 0
    rows, channels = y_ref.shape
    active = flag_ref[0] == 1
    heads = dt_ref.shape[1]
    dim = channels // heads
    half = STATE
    devices = rows // (micro * group_rows)
    head = groups_ref[0]
    block = ring.shape[2]
    blocks = w_ref.shape[1] // block

    def fetch(i):
        slot = lax.rem(i, slots)
        cols = pl.ds(pl.multiple_of(i * block, block), block)
        return pltpu.make_async_copy(w_ref.at[:, cols], ring.at[slot], sems.at[slot])

    loads = [pltpu.make_async_copy(const_ref, const, own_sems.at[0]), pltpu.make_async_copy(state_ref, state_buf, own_sems.at[1])]
    for copy in loads:
        copy.start()
    for i in range(min(slots, blocks)):
        fetch(i).start()

    @pl.when(groups_ref[0] >= 0)
    def _():
        arrived = dot(here_ref[...], place_columns(head, 0, devices)) + dot(over_ref[...], place_columns(head, 1, devices))
        pad_bc[8:, :] = arrived
        gather = gather_order(head, rows, micro, group_rows)
        loads[0].wait()
        bc = conv_silu(pad_bc, const, 2 * taps, taps)
        b_mat, c_mat = bc[:, :half], bc[:, half:]
        b_bf, c_bf = b_mat.astype(BF), c_mat.astype(BF)
        b_buf[...] = b_bf
        contract = (((1,), (1,)), ((), ()))
        scores = lax.dot_general(c_mat, b_mat, contract, precision=HIGHEST, preferred_element_type=F32)
        t_ids = lax.broadcasted_iota(jnp.int32, (rows, rows), 0)
        s_ids = lax.broadcasted_iota(jnp.int32, (rows, rows), 1)
        causal = t_ids >= s_ids
        scores = jnp.where(causal, scores, 0.0)

        raw = dot(gather.astype(F32), dt_ref[...], precision=HIGHEST) + const[4 * taps - 1:4 * taps, :heads]
        step = jnp.maximum(raw, 0.0) + jnp.log1p(jnp.exp(-jnp.abs(raw)))
        log_decay = dot(causal.astype(F32), -step * const[4 * taps:4 * taps + 1, :heads], precision=HIGHEST)
        end_log = log_decay[rows - 1:rows, :]
        end_buf[...] = jnp.exp(end_log)
        part_head, channel = iotas(3 * heads, channels)
        spread = (bits(part_head, 1, heads) == (channel >> (dim.bit_length() - 1))).astype(F32).astype(BF)
        step_full = spread_exact(step, spread)
        to_end_full = spread_exact(jnp.exp(end_log - log_decay), spread)
        decay_full = spread_exact(jnp.exp(log_decay), spread)
        log_rows = log_decay.T

        in_time(gather, groups_ref, group_rows, x_ref, pad_x)
        x_conv = conv_silu(pad_x, const, 0, taps)
        stepped = x_conv * step_full
        scaled[...] = stepped.astype(BF)
        weighted_buf[...] = (stepped * to_end_full).astype(BF)
        for j in range(heads):
            gap = jnp.minimum(log_decay[:, j:j + 1] - log_rows[j:j + 1, :], 0.0)
            weight = (scores * jnp.exp(gap)).astype(BF)
            cols = slice(j * dim, (j + 1) * dim)
            pad_x[8:, cols] = const[2 * taps - 1:2 * taps, cols] * x_conv[:, cols] + dot(weight, scaled[:, cols])

        loads[1].wait()
        state = state_buf[...].reshape(channels, half).astype(BF)
        carried = lax.dot_general(c_bf, state, contract, preferred_element_type=F32)
        y_ref[...] = (pad_x[8:, :] + carried * decay_full).astype(BF)

    kept = [
        pltpu.make_async_copy(src, dst, own_sems.at[i])
        for i, (src, dst) in enumerate(((weighted_buf, weighted_ref), (b_buf, b_ref), (end_buf, end_ref)))
    ]

    @pl.when(active)
    def _():
        for copy in kept:
            copy.start()

    sorted_ref[...] = dot(scatter_order(head, rows, micro, group_rows), y_ref[...]).astype(BF)
    size = rows // 2

    @pl.loop(0, blocks)
    def _(i):
        fetch(i).wait()
        part = dot(sorted_ref[...], ring[lax.rem(i, slots)]).astype(BF)
        cols = pl.ds(pl.multiple_of(i * block, block), block)
        for q, piece in enumerate(pieces):
            piece[:, cols] = part[q * size:(q + 1) * size, :]

        @pl.when(i + slots < blocks)
        def _():
            fetch(i + slots).start()

    @pl.when(active)
    def _():
        for copy in kept:
            copy.wait()


def scan_and_out(micro, group_rows, taps, groups, flag, x_proj, here, over, dt_raw, const, state, kept, old, w_out):
    rows, channels = x_proj.shape
    width = w_out.shape[1]
    block, slots = OUT_COLS, SLOTS
    far = [pltpu.with_memory_space_constraint(a, pltpu.HBM) for a in (const, state, w_out, *old)]
    shapes = [jax.ShapeDtypeStruct((rows // 2, width), BF)] * 2 + list(kept)
    vmem = pl.BlockSpec(memory_space=pltpu.VMEM)
    smem = pl.BlockSpec(memory_space=pltpu.SMEM)
    hbm = pl.BlockSpec(memory_space=pl.ANY)
    return pl.pallas_call(
        functools.partial(scan_kernel, micro, group_rows, slots, taps, len(old)),
        in_specs=[smem, smem] + [vmem] * 4 + [hbm] * (3 + len(old)),
        out_specs=[vmem] * 2 + [hbm] * 3,
        out_shape=shapes,
        input_output_aliases={9 + i: 2 + i for i in range(len(old))},
        scratch_shapes=[
            pltpu.VMEM((rows + 8, channels), F32),
            pltpu.VMEM((rows + 8, 2 * STATE), F32),
            pltpu.VMEM((rows, channels), BF),
            pltpu.VMEM((rows, channels), BF),
            pltpu.VMEM((rows, channels), BF),
            pltpu.VMEM(const.shape, F32),
            pltpu.VMEM(state.shape, F32),
            *[pltpu.VMEM(o.shape, o.dtype) for o in kept],
            pltpu.VMEM((slots, channels, block), BF),
            pltpu.SemaphoreType.DMA((slots,)),
            pltpu.SemaphoreType.DMA((3,)),
        ],
        compiler_params=params(SCAN_MIB),
        cost_estimate=cost(2 * rows * channels * (rows + STATE + width), 2 * w_out.size),
    )(groups, flag, x_proj, here, over, dt_raw, *far)


def state_kernel(end_ref, weighted_ref, b_ref, state_ref, value_ref, out_ref, copy_ref):
    heads, dim, _ = state_ref.shape
    copy_ref[...] = value_ref[...]
    added = lax.dot_general(
        weighted_ref[...], b_ref[...], (((0,), (0,)), ((), ())), preferred_element_type=F32
    )
    for j in range(heads):
        out_ref[j] = end_ref[0, j] * state_ref[j] + added[j * dim:(j + 1) * dim, :]


def state_update(end, weighted, b_mat, state, value):
    vmem = pl.BlockSpec(memory_space=pltpu.VMEM)
    return pl.pallas_call(
        state_kernel,
        in_specs=[pl.BlockSpec(memory_space=pltpu.SMEM)] + [vmem] * 4,
        out_specs=[vmem, vmem],
        out_shape=[jax.ShapeDtypeStruct(state.shape, F32), jax.ShapeDtypeStruct(value.shape, value.dtype)],
        compiler_params=params(12),
        cost_estimate=cost(2 * weighted.size * b_mat.shape[1], 8 * state.size),
    )(end, weighted, b_mat, state, value)


def rms_rows(rows_in, gain):
    floats = rows_in.astype(F32)
    scaled = floats * lax.rsqrt(jnp.mean(floats * floats, axis=-1, keepdims=True) + 1e-05)
    return (scaled * gain[None, :]).astype(BF)


def per_device(hidden, norm_gain, w_x, w_bc, w_dt, conv_x, conv_bc, dt_bias, a_rate, d_skip, w_out,
               ssm_init, conv_x_init, conv_bc_init):
    segment = lax.axis_index("pipe")
    segments = lax.axis_size("pipe")
    head = lax.axis_index("head")
    devices = lax.axis_size("head")
    chips = devices // 2
    micro, local, width = hidden.shape
    own_rows = micro * local
    rows = own_rows * devices
    half = rows // 2
    local_heads = dt_bias.shape[1]
    channels = w_x.shape[2]
    bc_cols = w_bc.shape[2]
    span = bc_cols // GROUPS

    everyone = jnp.arange(devices)
    distance = (ring_place(head // 2, chips) - ring_place(everyone // 2, chips)) % chips
    place = ((everyone ^ head) % 2) * chips + distance
    groups = (place[None, :] * micro + jnp.arange(micro)[:, None]).reshape(-1)
    groups = jnp.concatenate([head[None], groups]).astype(jnp.int32)

    my_group = head * GROUPS // devices
    tail_bc = lax.dynamic_index_in_dim(conv_bc_init[0].reshape(-1, 2 * STATE, GROUPS), my_group, 2, keepdims=False)
    taps_bc = lax.dynamic_index_in_dim(conv_bc[0].reshape(-1, 2 * STATE, GROUPS), my_group, 2, keepdims=False)
    skip = jnp.repeat(d_skip[0], channels // local_heads)[None, :]

    taps = conv_x.shape[1]
    const_cols = max(channels, 2 * STATE)

    def wide(values):
        return jnp.pad(values, ((0, 0), (0, const_cols - values.shape[1])))

    const = jnp.concatenate([
        wide(a) for a in (conv_x_init[0], conv_x[0], skip, tail_bc, taps_bc, dt_bias, a_rate)
    ])
    const = jnp.pad(const, ((0, -const.shape[0] % 8), (0, 0)))

    block = 256 if channels >= 2048 else 128
    count = channels // block
    kept = min(HELD, count)
    in_sum = min(SUM_LOADS, kept)
    inner_plan = [(w_x[0], block, i) for i in range(kept)]
    go = groups

    current = hidden.reshape(own_rows, width)
    out_rows = jnp.zeros((own_rows, width), BF)
    parts = (
        jax.ShapeDtypeStruct((rows, channels), BF),
        jax.ShapeDtypeStruct((rows, STATE), BF),
        jax.ShapeDtypeStruct((1, local_heads), F32),
    )
    old = []
    bc_plan = [(w_bc[0], 256, i) for i in range(bc_cols // 256)] if BC_HELD else []
    held, held_bc = [], []
    for tick in range(segments):
        last = tick + 1 == segments
        active = segment == tick
        flag = active.astype(jnp.int32).reshape(1)
        normed = rms_rows(current, norm_gain[0])
        arrived = [ring_shift(normed, s) for s in range(1, chips)]
        if tick:
            more, normed = load_beside(go, inner_plan[in_sum:] + bc_plan, normed)
            held, held_bc = held + more[:kept - in_sum], more[kept - in_sum:]
        pieces = [normed] + arrived
        if own_rows % 16:
            pieces = [jnp.concatenate(pieces, axis=0)]
        pieces = pieces + [core_swap(piece) for piece in pieces]
        normed_all, dt_raw, bc_out = project_first(
            go, pieces, micro, local, w_bc[0], w_dt[0].T, held_bc, () if tick else (const,)
        )
        bc_parts = [bc_out[:, s * 2 * span:(s + 1) * 2 * span] for s in range(chips)]
        bc_here = bc_parts[0]
        bc_parts = [ring_shift(bc_parts[s], s) for s in range(1, chips)]
        x_proj, bc_here = held_inner(go, normed_all, held, w_x[0], block, bc_here)
        bc_here = join([bc_here] + bc_parts)
        mine, other, *old = scan_and_out(
            micro, local, taps, groups, flag, x_proj, bc_here, core_swap(bc_here), dt_raw, const, ssm_init[0], parts, old,
            w_out[0],
        )
        received = core_swap(other)
        pair = (mine.astype(F32) + received.astype(F32)).astype(BF)
        arrived = [ring_shift(pair[s * own_rows:(s + 1) * own_rows], s) for s in range(1, chips)]
        own = pair[:own_rows]
        if last:
            state_out, own = state_update(old[2], old[0], old[1], ssm_init[0], own)
        else:
            held, own = load_beside(go, inner_plan[:in_sum], own)
        total = own.astype(F32)
        for piece in arrived:
            total = total + piece.astype(F32)
        new_rows = (current.astype(F32) + total).astype(BF)
        out_rows = jnp.where(active, new_rows, out_rows)
        if not last:
            current = next_segment(new_rows, tick)
    return (out_rows.reshape(1, micro, local, width), state_out[None])


def solution(mesh):
    in_specs = (
        P(None, "head", None),
        P("pipe", None),
        P("pipe", None, "head"),
        P("pipe", None, "head"),
        P("pipe", None, "head"),
        P("pipe", None, "head"),
        P("pipe", None, None),
        P("pipe", "head"),
        P("pipe", "head"),
        P("pipe", "head"),
        P("pipe", "head", None),
        P("pipe", "head", None, None),
        P("pipe", None, "head"),
        P("pipe", None, None),
    )
    out_specs = (P("pipe", None, "head", None), P("pipe", "head", None, None))
    return jax.shard_map(
        per_device, mesh=mesh, in_specs=in_specs, out_specs=out_specs, check_vma=False
    )
```
